128 devices in a mesh: row: 8 (over x, core), col: 16 (over y, z).
Axes of the slice: x: 4, y: 4, z: 4, core: 2. Of those that a mesh axis runs over, the one named last changes fastest.
Arguments:
- elevation: float32 [1024, 65536], P('row', 'col'), may hold values from -6 to 6
- row_spectra: float32 [2, 2, 1024], replicated, may hold values from -4 to 4, as said below
- col_spectra: float32 [2, 2, 65536], replicated, may hold values from -4 to 4, as said below
Outputs:
- correlations: float32 [2, 1024, 65536], P(None, 'row', 'col')
The draws below stay inside these ranges and needn't reach their ends.
Inputs may be any that keep to these rules, and one draw needn't show every extreme that they name: `row_spectra`: each footprint's row spectrum is that of a real profile: entry 1024 - k is the complex conjugate of entry k. `col_spectra`: each footprint's column spectrum is that of a real profile: entry 65536 - k is the complex conjugate of entry k.
All inputs are finite; a program needn't handle non-finite values.
Results may differ from the reference program's by a relative error of at most 0.0001.
Values sent between devices are 32-bit elements; how exact they have to be, the bound alone decides.
A program may use at most 192 MiB of HBM per device.

```python
import jax
import jax.numpy as jnp

COLS = 65536
FOOT = 2
ROWS = 1024


def symmetric_spectrum(raw_real, raw_imag):
    mirror_real = jnp.roll(jnp.flip(raw_real, -1), 1, -1)
    mirror_imag = jnp.roll(jnp.flip(raw_imag, -1), 1, -1)
    return jnp.stack([0.5 * (raw_real + mirror_real), 0.5 * (raw_imag - mirror_imag)], axis=1)


def draw_row_spectra(key, part):
    key = jax.random.fold_in(key, 11)
    raw_values = jnp.clip(jax.random.normal(key, (2, FOOT, ROWS), jnp.float32), -4.0, 4.0)
    return symmetric_spectrum(raw_values[0], raw_values[1])


def draw_col_spectra(key, part):
    key = jax.random.fold_in(key, 12)
    raw_values = jnp.clip(jax.random.normal(key, (2, FOOT, COLS), jnp.float32), -4.0, 4.0)
    return symmetric_spectrum(raw_values[0], raw_values[1])


def block_levels(key, dims, split, least, high):
    loudness = 1.0
    for dim, blocks in split:
        heights = jax.random.uniform(jax.random.fold_in(jax.random.fold_in(key, 6), dim), (blocks,), jnp.float32, least / len(split), high / len(split))
        loudness = loudness * jnp.repeat(jnp.exp(heights), dims[dim] // blocks).reshape((-1,) + (1,) * (len(dims) - 1 - dim))
    return loudness


def noise(key, shape, spread, limit, split=(), kind=jnp.bfloat16):
    loudness = block_levels(key, shape, split, -0.22, 0.18) if split else 1.0
    drawn = jax.random.normal(key, shape, jnp.float32) * spread * loudness
    return jnp.minimum(jnp.maximum(drawn, -limit), limit).astype(kind)


def setup_inputs(seed: int = 0) -> dict:
    key_list = jax.random.split(jax.random.key(seed), 4)
    return {
        "elevation": noise(key_list[0], (ROWS, COLS), 1.0, 6.0, ((0, 8), (1, 16)), jnp.float32),
        "row_spectra": draw_row_spectra(jax.random.fold_in(key_list[3], 71), 0),
        "col_spectra": draw_col_spectra(jax.random.fold_in(key_list[3], 71), 0),
    }


def reference(elevation, row_spectra, col_spectra):
    spectrum = jnp.fft.fft2(elevation)
    correlations = []
    for footprint in range(FOOT):
        row_gain = row_spectra[footprint, 0] + 1j * row_spectra[footprint, 1]
        col_gain = col_spectra[footprint, 0] + 1j * col_spectra[footprint, 1]
        product = spectrum * row_gain[:, None] * col_gain[None, :]
        correlations.append(jnp.real(jnp.fft.ifft2(product)))
    return jnp.stack(correlations)
```

```python
import math

import jax
import jax.numpy as jnp
import ml_dtypes
import numpy as np
from jax import lax
from jax.experimental import pallas as pl
from jax.experimental.pallas import tpu as pltpu
from jax.sharding import PartitionSpec as P

MESH = pl.DeviceIdType.MESH
SIDE = 256
ROW_DEVICES = 8
COL_DEVICES = 16
ROWS = 1024
LOCAL_COLS = 4096
LANES = 128
BLOCKS = LOCAL_COLS // LANES
TILES = ROWS // ROW_DEVICES // 8
SLOTS = BLOCKS // ROW_DEVICES
YZ_STEPS = [(dy, dz) for dy in range(4) for dz in range(4) if (dy, dz) != (0, 0)]
X_STEPS = [(dx, dk) for dx in range(4) for dk in range(2) if (dx, dk) != (0, 0)]


def split_constant(values):
    high = values.astype(ml_dtypes.bfloat16)
    low = (values - high.astype(np.float64)).astype(ml_dtypes.bfloat16)
    return high, low


def dft_constants():
    index = np.arange(SIDE)
    angles = 2.0 * np.pi / SIDE * (np.outer(index, index) % SIDE)
    cos, sin = np.cos(angles), np.sin(angles)
    left = np.block([[cos, sin], [-sin, cos]])
    right = np.block([[cos, -sin], [sin, cos]])
    turn = 2.0 * np.pi / (SIDE * SIDE) * np.outer(index, index)
    return split_constant(left) + split_constant(right) + (
        np.cos(turn).astype(np.float32),
        np.sin(turn).astype(np.float32),
    )


def split(values):
    high = values.astype(jnp.bfloat16)
    low = (values - high.astype(jnp.float32)).astype(jnp.bfloat16)
    return high, low


def dot(left, right):
    return jnp.dot(left, right, preferred_element_type=jnp.float32)


def dot_split(left, right):
    return dot(left[0], right[0]) + (dot(left[1], right[0]) + dot(left[0], right[1]))


def kernel(
    elev, profiles, gains, fwd_hi, fwd_lo, inv_hi, inv_lo, turn_cos, turn_sin, out,
    mid, yz_in, yz_res, x_in, x_res, circ_hi, circ_lo, x_hi, x_lo,
    yz_send, yz_recv, x_send, x_recv, own_sem,
):
    row, col = lax.axis_index("row"), lax.axis_index("col")

    def yz_peer(step):
        y = lax.rem(col // 4 + step[0], 4)
        z = lax.rem(col % 4 + step[1], 4)
        return y * 4 + z

    def x_peer(step):
        return lax.rem(row // 2 + step[0], 4) * 2 + lax.rem(row % 2 + step[1], 2)

    barrier = pltpu.get_barrier_semaphore()
    for step in YZ_STEPS:
        pl.semaphore_signal(barrier, inc=1, device_id=(row, yz_peer(step)), device_id_type=MESH)
    for step in X_STEPS:
        pl.semaphore_signal(barrier, inc=1, device_id=(x_peer(step), col), device_id_type=MESH)
    pl.semaphore_wait(barrier, len(YZ_STEPS) + len(X_STEPS))

    def yz_copies(half, stage, source, target):
        return [
            pltpu.make_async_remote_copy(
                src_ref=source(yz_peer(step)), dst_ref=target,
                send_sem=yz_send.at[half, stage, i], recv_sem=yz_recv.at[half, stage, i],
                device_id=(row, yz_peer(step)), device_id_type=MESH,
            )
            for i, step in enumerate(YZ_STEPS)
        ]

    def x_copies(half, stage, source, target):
        return [
            pltpu.make_async_remote_copy(
                src_ref=source(x_peer(step)), dst_ref=target,
                send_sem=x_send.at[half, stage, i], recv_sem=x_recv.at[half, stage, i],
                device_id=(x_peer(step), col), device_id_type=MESH,
            )
            for i, step in enumerate(X_STEPS)
        ]

    def start(copies):
        for copy in copies:
            copy.start()

    def wait_recv(copies):
        for copy in copies:
            copy.wait_recv()

    def build_circulant(half):
        spread = jnp.broadcast_to(profiles[1 - half], (128, ROWS))
        high, low = split(pltpu.roll(spread, 0, 1, stride=1, stride_axis=0))
        circ_hi[...] = high
        circ_lo[...] = low

    def row_filter(half):
        for slot in range(SLOTS):
            lanes = slice(slot * LANES, (slot + 1) * LANES)
            high, low = split(x_in[half, :, :, slot].reshape(ROWS, LANES))
            for base in (0, ROWS):
                x_hi[base:base + ROWS, lanes] = high
                x_lo[base:base + ROWS, lanes] = low

        def block(i, carry):
            rows = pl.ds(pl.multiple_of(i * 128, 128), ROWS)
            result = dot_split((circ_hi[...], circ_lo[...]), (x_hi[rows, :], x_lo[rows, :]))
            for slot in range(SLOTS):
                x_res[half, i, :, slot] = result[:, slot * LANES:(slot + 1) * LANES].reshape(TILES, 8, LANES)
            return carry

        lax.fori_loop(0, ROW_DEVICES, block, 0)

    def col_filter(half):
        source = yz_in.at[half].reshape(SIDE * 16, LANES)
        result = yz_res.at[half].reshape(SIDE * 16, LANES)
        forward = (fwd_hi, fwd_lo)
        inverse = (inv_hi, inv_lo)

        def whole(pair):
            return pair[0][...], pair[1][...]

        def load_row(row_id):
            return jnp.concatenate(
                [source[pl.ds(8 * side + row_id, SIDE, stride=16), :] for side in range(2)], 1
            )

        def store_row(row_id, values):
            for side in range(2):
                result[pl.ds(8 * side + row_id, SIDE, stride=16), :] = values[:, side * LANES:(side + 1) * LANES]

        for pair in range(4):
            field = jnp.concatenate([load_row(2 * pair), load_row(2 * pair + 1)], 0)
            first = dot_split(whole(forward), split(field))
            real, imag = first[:SIDE], first[SIDE:]
            cos, sin = turn_cos[...], turn_sin[...]
            turned = jnp.concatenate([real * cos + imag * sin, imag * cos - real * sin], 1)
            second = dot_split(split(turned), whole(inverse))
            real, imag = second[:, :SIDE], second[:, SIDE:]
            gain_real, gain_imag = gains[half, 0], gains[half, 1]
            scaled = jnp.concatenate(
                [real * gain_real - imag * gain_imag, real * gain_imag + imag * gain_real], 1
            )
            third = dot_split(split(scaled), whole(forward))
            real, imag = third[:, :SIDE], third[:, SIDE:]
            turned = jnp.concatenate([real * cos - imag * sin, imag * cos + real * sin], 0)
            fourth = dot_split(whole(inverse), split(turned))
            store_row(2 * pair, fourth[:SIDE])
            store_row(2 * pair + 1, fourth[SIDE:])

    started = []
    for half in range(2):
        col_field = elev if half == 0 else mid.at[1]
        row_field = elev if half == 0 else mid.at[0]
        col_target = mid.at[0] if half == 0 else out.at[1]
        row_target = mid.at[1] if half == 0 else out.at[0]
        mine = pl.ds(SLOTS * row, SLOTS)

        ins_yz = yz_copies(half, 0, lambda peer: col_field.at[peer], yz_in.at[half, col])
        ins_x = x_copies(
            half, 0, lambda peer: row_field.at[:, pl.ds(SLOTS * peer, SLOTS)], x_in.at[half, row]
        )
        own_yz = pltpu.make_async_copy(col_field.at[col], yz_in.at[half, col], own_sem.at[half, 0])
        own_x = pltpu.make_async_copy(row_field.at[:, mine], x_in.at[half, row], own_sem.at[half, 1])
        start(ins_yz + ins_x + [own_yz, own_x])
        build_circulant(half)
        own_x.wait()
        wait_recv(ins_x)
        row_filter(half)
        outs_x = x_copies(half, 1, lambda peer: x_res.at[half, peer], row_target.at[:, mine])
        back_x = pltpu.make_async_copy(x_res.at[half, row], row_target.at[:, mine], own_sem.at[half, 2])
        start(outs_x + [back_x])
        own_yz.wait()
        wait_recv(ins_yz)
        col_filter(half)
        outs_yz = yz_copies(half, 1, lambda peer: yz_res.at[half, peer], col_target.at[col])
        back_yz = pltpu.make_async_copy(yz_res.at[half, col], col_target.at[col], own_sem.at[half, 3])
        start(outs_yz + [back_yz])
        back_x.wait()
        wait_recv(outs_x)
        back_yz.wait()
        wait_recv(outs_yz)
        started += ins_yz + ins_x + outs_x + outs_yz
    for copy in started:
        copy.wait_send()


def row_profiles(row_spectra):
    side = 32
    index = np.arange(side)
    inner = 2.0 * np.pi / side * (np.outer(index, index) % side)
    cos, sin = np.cos(inner).astype(np.float32), np.sin(inner).astype(np.float32)
    turn = 2.0 * np.pi / ROWS * np.outer(index, index)
    turn_cos, turn_sin = np.cos(turn).astype(np.float32), np.sin(turn).astype(np.float32)
    folded = row_spectra.reshape(2, 2, side, side)

    def product(form, left, right):
        return jnp.einsum(form, left, right, precision=lax.Precision.HIGHEST)

    real, imag = folded[:, 0], folded[:, 1]
    first_real = product("fba,bj->faj", real, cos) + product("fba,bj->faj", imag, sin)
    first_imag = product("fba,bj->faj", imag, cos) - product("fba,bj->faj", real, sin)
    real = first_real * turn_cos + first_imag * turn_sin
    imag = first_imag * turn_cos - first_real * turn_sin
    values = product("faj,ai->fij", real, cos) + product("faj,ai->fij", imag, sin)
    return values.reshape(2, 1, ROWS) * (1.0 / ROWS)


def body(elevation, row_spectra, col_spectra):
    tiles = elevation.reshape(TILES, 8, BLOCKS, LANES).transpose(0, 2, 1, 3)
    profiles = row_profiles(row_spectra)
    gains = col_spectra.reshape(2, 2, SIDE, SIDE).transpose(0, 1, 3, 2) * (1.0 / (SIDE * SIDE))
    field = (TILES, BLOCKS, 8, LANES)
    slots = (ROW_DEVICES, TILES, SLOTS, 8, LANES)
    vmem = pl.BlockSpec(memory_space=pltpu.VMEM)
    result = pl.pallas_call(
        kernel,
        out_shape=jax.ShapeDtypeStruct((2,) + field, jnp.float32),
        in_specs=[vmem] * 9,
        out_specs=vmem,
        scratch_shapes=[
            pltpu.VMEM((2,) + field, jnp.float32),
            pltpu.VMEM((2,) + field, jnp.float32),
            pltpu.VMEM((2,) + field, jnp.float32),
            pltpu.VMEM((2,) + slots, jnp.float32),
            pltpu.VMEM((2,) + slots, jnp.float32),
            pltpu.VMEM((128, ROWS), jnp.bfloat16),
            pltpu.VMEM((128, ROWS), jnp.bfloat16),
            pltpu.VMEM((2 * ROWS, SLOTS * SIDE), jnp.bfloat16),
            pltpu.VMEM((2 * ROWS, SLOTS * SIDE), jnp.bfloat16),
            pltpu.SemaphoreType.DMA((2, 2, len(YZ_STEPS))),
            pltpu.SemaphoreType.DMA((2, 2, len(YZ_STEPS))),
            pltpu.SemaphoreType.DMA((2, 2, len(X_STEPS))),
            pltpu.SemaphoreType.DMA((2, 2, len(X_STEPS))),
            pltpu.SemaphoreType.DMA((2, 4)),
        ],
        compiler_params=pltpu.CompilerParams(
            collective_id=0, has_side_effects=True, vmem_limit_bytes=58 * 2**20
        ),
    )(tiles, profiles, gains, *(jnp.asarray(table) for table in dft_constants()))
    return result.transpose(0, 1, 3, 2, 4).reshape((2,) + elevation.shape)


def solution(mesh):
    in_specs = (P("row", "col"), P(), P())
    out_specs = P(None, "row", "col")
    return jax.shard_map(body, mesh=mesh, in_specs=in_specs, out_specs=out_specs, check_vma=False)
```

```python
import ml_dtypes
import jax
import jax.numpy as jnp
import numpy as np
from jax import lax
from jax.experimental import pallas as pl
from jax.experimental.pallas import tpu as pltpu
from jax.sharding import PartitionSpec as P

MESH = pl.DeviceIdType.MESH
SIDE = 256
LANES = 128
ROW_DEVICES = 8
COL_DEVICES = 16
ROWS = 1024
LOCAL_COLS = 4096
BLOCKS = LOCAL_COLS // LANES
TILES = ROWS // ROW_DEVICES // 8
PARTS = 2
SLOTS = BLOCKS // ROW_DEVICES // PARTS
LINES = 8 // PARTS
HALVES = SIDE // LANES
STRIPS = LOCAL_COLS // SIDE
YZ_STEPS = [
    (1, 1), (3, 3), (2, 2), (1, 3), (3, 1), (2, 1), (1, 2), (2, 3),
    (3, 2), (2, 0), (0, 2), (1, 0), (0, 1), (3, 0), (0, 3),
]
X_STEPS = [(1, 0), (3, 0), (1, 1), (3, 1), (2, 0), (2, 1), (0, 1)]


def split_constant(values):
    high = values.astype(ml_dtypes.bfloat16)
    low = (values - high.astype(np.float64)).astype(ml_dtypes.bfloat16)
    return [high, low]


def dft_constants():
    index = np.arange(SIDE)
    angles = 2.0 * np.pi / SIDE * (np.outer(index, index) % SIDE)
    cos, sin = np.cos(angles), np.sin(angles)
    forward = np.block([[cos, sin], [-sin, cos]])
    inverse = np.block([[cos, -sin], [sin, cos]])
    matrices = np.stack(split_constant(forward) + split_constant(inverse))
    turn = 2.0 * np.pi / (SIDE * SIDE) * np.outer(index, index)
    turns = np.stack([np.cos(turn), np.sin(turn)]).astype(np.float32)
    low = np.arange(8)
    lane = np.arange(LANES)
    first = 2.0 * np.pi / ROWS * (
        low[None, :, None] * (LANES * low[:, None, None] + lane[None, None, :]) % ROWS
    )
    first = np.stack([np.cos(first), np.sin(first)]).astype(np.float32)
    second = 2.0 * np.pi / LANES * (np.outer(lane, lane) % LANES)
    second = (np.stack([np.cos(second), np.sin(second)]) / ROWS).astype(np.float32)
    return matrices, turns, first, second


def split(values):
    high = values.astype(jnp.bfloat16)
    low = (values - high.astype(jnp.float32)).astype(jnp.bfloat16)
    return high, low


def dot(left, right):
    return jnp.dot(left, right, preferred_element_type=jnp.float32)


def dot_precise(left, right):
    return jnp.dot(
        left, right, preferred_element_type=jnp.float32, precision=lax.Precision.HIGHEST
    )


def dot_split(left, right):
    return dot(left[0], right[0]) + (dot(left[1], right[0]) + dot(left[0], right[1]))


def interleave(first, second):
    merged = []
    count = max(len(first), len(second))
    for i in range(count):
        for member in (first, second):
            merged += member[len(member) * i // count:len(member) * (i + 1) // count]
    return merged


def kernel(
    elev_hbm, row_hbm, col_hbm, matrices_hbm, turns_hbm, first_hbm, second_hbm,
    out_row, out_col,
    elev, row_spec, col_spec, matrices, turns, first, second, gains, circ_hi, circ_lo,
    yz_pack, yz_in, yz_res, yz_mid, col_mid, x_in, x_res, row_mid, x_hi, x_lo,
    yz_send, yz_recv, x_send, x_recv, own_sem, load_sem,
):
    row, col = lax.axis_index("row"), lax.axis_index("col")

    def yz_peer(step):
        return lax.rem(col // 4 + step[0], 4) * 4 + lax.rem(col % 4 + step[1], 4)

    def x_peer(step):
        return lax.rem(row // 2 + step[0], 4) * 2 + lax.rem(row % 2 + step[1], 2)

    loads = [
        pltpu.make_async_copy(source, target, load_sem.at[i])
        for i, (source, target) in enumerate([
            (elev_hbm, elev), (row_hbm, row_spec), (first_hbm, first), (second_hbm, second),
            (col_hbm, col_spec), (matrices_hbm, matrices), (turns_hbm, turns),
        ])
    ]
    for load in loads:
        load.start()

    barrier = pltpu.get_barrier_semaphore()
    for step in YZ_STEPS:
        pl.semaphore_signal(barrier, inc=1, device_id=(row, yz_peer(step)), device_id_type=MESH)
    for step in X_STEPS:
        pl.semaphore_signal(barrier, inc=1, device_id=(x_peer(step), col), device_id_type=MESH)

    def yz_copies(half, stage, part, source, target):
        return [
            pltpu.make_async_remote_copy(
                src_ref=source(yz_peer(step)), dst_ref=target,
                send_sem=yz_send.at[half, stage, part, i], recv_sem=yz_recv.at[half, stage, part, i],
                device_id=(row, yz_peer(step)), device_id_type=MESH,
            )
            for i, step in enumerate(YZ_STEPS)
        ]

    def x_copies(half, stage, part, source, target):
        return [
            pltpu.make_async_remote_copy(
                src_ref=source(x_peer(step)), dst_ref=target,
                send_sem=x_send.at[half, stage, part, i], recv_sem=x_recv.at[half, stage, part, i],
                device_id=(x_peer(step), col), device_id_type=MESH,
            )
            for i, step in enumerate(X_STEPS)
        ]

    def start(copies):
        for copy in copies:
            copy.start()

    def wait_recv(copies):
        for copy in copies:
            copy.wait_recv()

    def lines(part):
        for line in range(LINES):
            for side in range(HALVES):
                yield line, side, pl.ds(8 * side + LINES * part + line, SIDE, stride=8 * HALVES)

    def pack(field, half, part):
        rows = field.reshape(SIDE * 8 * HALVES, LANES)
        for line, side, where in lines(part):
            yz_pack[half, part, :, line, side] = rows[where, :].reshape(COL_DEVICES, STRIPS, LANES)

    def unpack(part):
        rows = col_mid.reshape(SIDE * 8 * HALVES, LANES)
        for line, side, where in lines(part):
            rows[where, :] = yz_mid[part, :, line, side].reshape(SIDE, LANES)

    def build_circulant(foot):
        real = row_spec[foot, pl.ds(0, 8, stride=2), :]
        imag = row_spec[foot, pl.ds(1, 8, stride=2), :]
        turned_real = jnp.zeros((8, LANES), jnp.float32)
        turned_imag = jnp.zeros((8, LANES), jnp.float32)
        for i in range(8):
            cos, sin = first[0, i], first[1, i]
            turned_real += real[i:i + 1] * cos + imag[i:i + 1] * sin
            turned_imag += imag[i:i + 1] * cos - real[i:i + 1] * sin
        grid = dot_precise(turned_real, second[0]) + dot_precise(turned_imag, second[1])
        index = lax.broadcasted_iota(jnp.int32, (LANES, ROWS), 1)
        group = lax.broadcasted_iota(jnp.int32, (LANES, ROWS), 0)
        spread = dot_precise(grid, jnp.where(index // 8 == group, 1.0, 0.0))
        keep = index[:8] % 8 == group[:8]
        profile = jnp.sum(jnp.where(keep, spread, 0.0), axis=0, keepdims=True)
        rolled = pltpu.roll(jnp.broadcast_to(profile, (LANES, ROWS)), 0, 1, stride=1, stride_axis=0)
        circ_hi[foot], circ_lo[foot] = split(rolled)

    def build_gains(foot):
        for member in range(2):
            for side in range(HALVES):
                values = col_spec[foot, pl.ds(2 * side + member, SIDE, stride=4), :]
                gains[foot, member, side * LANES:(side + 1) * LANES, :] = values.T * (1.0 / (SIDE * SIDE))

    def row_filter(half, part, send):
        foot = 1 - half
        for slot in range(SLOTS):
            lanes = slice(slot * LANES, (slot + 1) * LANES)
            high, low = split(x_in[half, part, :, :, slot].reshape(ROWS, LANES))
            for base in (0, ROWS):
                x_hi[base:base + ROWS, lanes] = high
                x_lo[base:base + ROWS, lanes] = low
        for owner, copy in send:
            rows = pl.ds(pl.multiple_of(owner * LANES, LANES), ROWS)
            result = dot_split((circ_hi[foot], circ_lo[foot]), (x_hi[rows, :], x_lo[rows, :]))
            for slot in range(SLOTS):
                x_res[half, part, owner, :, slot] = result[:, slot * LANES:(slot + 1) * LANES].reshape(TILES, 8, LANES)
            copy.start()

    def col_filter(half, part):
        foot = half
        forward = (matrices[0], matrices[1])
        inverse = (matrices[2], matrices[3])
        cos, sin = turns[0], turns[1]
        gain_real, gain_imag = gains[foot, 0], gains[foot, 1]

        def load_line(line):
            return jnp.concatenate(
                [yz_in[half, part, :, line, side].reshape(SIDE, LANES) for side in range(HALVES)], 1
            )

        def store_line(line, values):
            for side in range(HALVES):
                yz_res[half, part, :, line, side] = values[:, side * LANES:(side + 1) * LANES].reshape(
                    COL_DEVICES, STRIPS, LANES
                )

        for line in range(0, LINES, 2):
            field = jnp.concatenate([load_line(line), load_line(line + 1)], 0)
            result = dot_split(forward, split(field))
            real, imag = result[:SIDE], result[SIDE:]
            field = jnp.concatenate([real * cos + imag * sin, imag * cos - real * sin], 1)
            result = dot_split(split(field), inverse)
            real, imag = result[:, :SIDE], result[:, SIDE:]
            field = jnp.concatenate(
                [real * gain_real - imag * gain_imag, real * gain_imag + imag * gain_real], 1
            )
            result = dot_split(split(field), forward)
            real, imag = result[:, :SIDE], result[:, SIDE:]
            field = jnp.concatenate([real * cos - imag * sin, imag * cos + real * sin], 0)
            result = dot_split(inverse, split(field))
            store_line(line, result[:SIDE])
            store_line(line + 1, result[SIDE:])

    started = []

    def row_part(part):
        return pl.ds(SLOTS * (PARTS * row + part), SLOTS)

    for half in range(2):
        first_half = half == 0
        row_field = elev if first_half else col_mid
        col_field = elev if first_half else row_mid
        row_target = row_mid if first_half else out_row
        col_target = yz_mid if first_half else out_col
        ins_yz, ins_x, own_yz, own_x = [], [], [], []
        for part in range(PARTS):
            ins_yz.append(yz_copies(
                half, 0, part, lambda peer: yz_pack.at[half, part, peer], yz_in.at[half, part, col]
            ))
            ins_x.append(x_copies(
                half, 0, part,
                lambda peer: row_field.at[:, pl.ds(SLOTS * (PARTS * peer + part), SLOTS)],
                x_in.at[half, part, row],
            ))
            own_yz.append(pltpu.make_async_copy(
                yz_pack.at[half, part, col], yz_in.at[half, part, col], own_sem.at[half, 0, part]
            ))
            own_x.append(pltpu.make_async_copy(
                row_field.at[:, row_part(part)], x_in.at[half, part, row], own_sem.at[half, 1, part]
            ))
        if first_half:
            loads[0].wait()
            for part in range(PARTS):
                pack(elev, half, part)
            pl.semaphore_wait(barrier, len(YZ_STEPS) + len(X_STEPS))
            for part in range(PARTS):
                start(interleave(ins_yz[part], ins_x[part]) + [own_yz[part], own_x[part]])
            for load in loads[1:]:
                load.wait()
            for foot in range(2):
                build_circulant(foot)
                build_gains(foot)
        else:
            back_yz[0].wait()
            wait_recv(outs_yz[0])
            unpack(0)
            for part in range(PARTS):
                back_x[part].wait()
                wait_recv(outs_x[part])
            for part in range(PARTS):
                pack(row_mid, half, part)
                start(ins_yz[part] + [own_yz[part]])
            back_yz[1].wait()
            wait_recv(outs_yz[1])
            unpack(1)
            for part in range(PARTS):
                start(ins_x[part] + [own_x[part]])

        outs_yz, outs_x, back_yz, back_x = [], [], [], []
        for part in range(PARTS):
            own_x[part].wait()
            wait_recv(ins_x[part])
            outs_x.append(x_copies(
                half, 1, part, lambda peer: x_res.at[half, part, peer], row_target.at[:, row_part(part)]
            ))
            back_x.append(pltpu.make_async_copy(
                x_res.at[half, part, row], row_target.at[:, row_part(part)], own_sem.at[half, 2, part]
            ))
            owners = [x_peer(step) for step in X_STEPS] + [row]
            row_filter(half, part, list(zip(owners, outs_x[part] + [back_x[part]])))

            own_yz[part].wait()
            wait_recv(ins_yz[part])
            col_filter(half, part)
            outs_yz.append(yz_copies(
                half, 1, part, lambda peer: yz_res.at[half, part, peer], col_target.at[part, col]
            ))
            back_yz.append(pltpu.make_async_copy(
                yz_res.at[half, part, col], col_target.at[part, col], own_sem.at[half, 3, part]
            ))
            start(outs_yz[part] + [back_yz[part]])
        for part in range(PARTS):
            started += ins_yz[part] + ins_x[part] + outs_yz[part] + outs_x[part]

    for part in range(PARTS):
        back_x[part].wait()
        wait_recv(outs_x[part])
        back_yz[part].wait()
        wait_recv(outs_yz[part])
    for copy in started:
        copy.wait_send()


def finish_kernel(row_ref, col_ref, out):
    tiles = row_ref.shape[0]
    out[0] = row_ref[...]
    rows = out.reshape(2 * tiles * BLOCKS * 8, LANES)
    for part in range(PARTS):
        for line in range(LINES):
            for side in range(HALVES):
                begin = tiles * BLOCKS * 8 + 8 * side + LINES * part + line
                rows[pl.ds(begin, tiles * STRIPS, stride=8 * HALVES), :] = col_ref[part, :, line, side].reshape(
                    tiles * STRIPS, LANES
                )


def body(elevation, row_spectra, col_spectra):
    tiles = elevation.reshape(TILES, 8, BLOCKS, LANES).transpose(0, 2, 1, 3)
    row_lines = row_spectra.reshape(2, 2, ROWS // LANES, LANES).transpose(0, 2, 1, 3)
    col_lines = col_spectra.reshape(2, 2, SIDE * HALVES, LANES).transpose(0, 2, 1, 3)
    inputs = [
        tiles,
        row_lines.reshape(2, 2 * ROWS // LANES, LANES),
        col_lines.reshape(2, 2 * SIDE * HALVES, LANES),
    ] + [jnp.asarray(table) for table in dft_constants()]
    field = (TILES, BLOCKS, 8, LANES)
    packed = (PARTS, COL_DEVICES, LINES, HALVES, STRIPS, LANES)
    slots = (PARTS, ROW_DEVICES, TILES, SLOTS, 8, LANES)
    anywhere = pl.BlockSpec(memory_space=pl.ANY)
    row_done, col_done = pl.pallas_call(
        kernel,
        out_shape=[jax.ShapeDtypeStruct(field, jnp.float32), jax.ShapeDtypeStruct(packed, jnp.float32)],
        in_specs=[anywhere] * len(inputs),
        out_specs=[anywhere] * 2,
        scratch_shapes=[pltpu.VMEM(member.shape, member.dtype) for member in inputs] + [
            pltpu.VMEM((2, 2, SIDE, SIDE), jnp.float32),
            pltpu.VMEM((2, LANES, ROWS), jnp.bfloat16),
            pltpu.VMEM((2, LANES, ROWS), jnp.bfloat16),
            pltpu.VMEM((2,) + packed, jnp.float32),
            pltpu.VMEM((2,) + packed, jnp.float32),
            pltpu.VMEM((2,) + packed, jnp.float32),
            pltpu.VMEM(packed, jnp.float32),
            pltpu.VMEM(field, jnp.float32),
            pltpu.VMEM((2,) + slots, jnp.float32),
            pltpu.VMEM((2,) + slots, jnp.float32),
            pltpu.VMEM(field, jnp.float32),
            pltpu.VMEM((2 * ROWS, SLOTS * LANES), jnp.bfloat16),
            pltpu.VMEM((2 * ROWS, SLOTS * LANES), jnp.bfloat16),
            pltpu.SemaphoreType.DMA((2, 2, PARTS, len(YZ_STEPS))),
            pltpu.SemaphoreType.DMA((2, 2, PARTS, len(YZ_STEPS))),
            pltpu.SemaphoreType.DMA((2, 2, PARTS, len(X_STEPS))),
            pltpu.SemaphoreType.DMA((2, 2, PARTS, len(X_STEPS))),
            pltpu.SemaphoreType.DMA((2, 4, PARTS)),
            pltpu.SemaphoreType.DMA((len(inputs),)),
        ],
        compiler_params=pltpu.CompilerParams(
            collective_id=0, has_side_effects=True, vmem_limit_bytes=58 * 2**20
        ),
    )(*inputs)
    steps = 4
    result = pl.pallas_call(
        finish_kernel,
        grid=(steps,),
        out_shape=jax.ShapeDtypeStruct((2,) + field, jnp.float32),
        in_specs=[
            pl.BlockSpec((TILES // steps,) + field[1:], lambda i: (i, 0, 0, 0)),
            pl.BlockSpec((PARTS, COL_DEVICES // steps) + packed[2:], lambda i: (0, i, 0, 0, 0, 0)),
        ],
        out_specs=pl.BlockSpec((2, TILES // steps) + field[1:], lambda i: (0, i, 0, 0, 0)),
    )(row_done, col_done)
    return result.transpose(0, 1, 3, 2, 4).reshape((2,) + elevation.shape)


def solution(mesh):
    in_specs = (P("row", "col"), P(), P())
    out_specs = P(None, "row", "col")
    return jax.shard_map(body, mesh=mesh, in_specs=in_specs, out_specs=out_specs, check_vma=False)
```

```python
import ml_dtypes
import jax
import jax.numpy as jnp
import numpy as np
from jax import lax
from jax.experimental import pallas as pl
from jax.experimental.pallas import tpu as pltpu
from jax.sharding import PartitionSpec as P

MESH = pl.DeviceIdType.MESH
SIDE = 256
LANES = 128
ROW_DEVICES = 8
COL_DEVICES = 16
ROWS = 1024
LOCAL_COLS = 4096
BLOCKS = LOCAL_COLS // LANES
TILES = ROWS // ROW_DEVICES // 8
PARTS = 2
SLOTS = BLOCKS // ROW_DEVICES // PARTS
LINES = 8 // PARTS
HALVES = SIDE // LANES
STRIPS = LOCAL_COLS // SIDE
PAIRS = TILES // PARTS
YZ_STEPS = [
    (1, 1), (3, 3), (2, 2), (1, 3), (3, 1), (2, 1), (1, 2), (2, 3),
    (3, 2), (2, 0), (0, 2), (1, 0), (0, 1), (3, 0), (0, 3),
]
X_STEPS = [(1, 0), (3, 0), (1, 1), (3, 1), (2, 0), (2, 1), (0, 1)]


def split_constant(values):
    high = values.astype(ml_dtypes.bfloat16)
    low = (values - high.astype(np.float64)).astype(ml_dtypes.bfloat16)
    return [high, low]


def dft_constants():
    index = np.arange(SIDE)
    angles = 2.0 * np.pi / SIDE * (np.outer(index, index) % SIDE)
    cos, sin = np.cos(angles), np.sin(angles)
    forward = np.block([[cos, sin], [-sin, cos]])
    inverse = np.block([[cos, -sin], [sin, cos]])
    matrices = np.stack(split_constant(forward) + split_constant(inverse))
    turn = 2.0 * np.pi / (SIDE * SIDE) * np.outer(index, index)
    turns = np.stack([np.cos(turn), np.sin(turn)]).astype(np.float32)
    low = np.arange(8)
    lane = np.arange(LANES)
    first = 2.0 * np.pi / ROWS * (
        low[None, :, None] * (LANES * low[:, None, None] + lane[None, None, :]) % ROWS
    )
    first = np.stack([np.cos(first), np.sin(first)]).astype(np.float32)
    second = 2.0 * np.pi / LANES * (np.outer(lane, lane) % LANES)
    second = (np.stack([np.cos(second), np.sin(second)]) / ROWS).astype(np.float32)
    return matrices, turns, first, second


def split(values):
    high = values.astype(jnp.bfloat16)
    low = (values - high.astype(jnp.float32)).astype(jnp.bfloat16)
    return high, low


def dot(left, right):
    return jnp.dot(left, right, preferred_element_type=jnp.float32)


def dot_precise(left, right):
    return jnp.dot(
        left, right, preferred_element_type=jnp.float32, precision=lax.Precision.HIGHEST
    )


def dot_split(left, right):
    return dot(left[0], right[0]) + (dot(left[1], right[0]) + dot(left[0], right[1]))


def interleave(first, second):
    merged = []
    count = max(len(first), len(second))
    for i in range(count):
        for member in (first, second):
            merged += member[len(member) * i // count:len(member) * (i + 1) // count]
    return merged


def kernel(
    elev_hbm, row_hbm, col_hbm, matrices_hbm, turns_hbm, first_hbm, second_hbm,
    out,
    elev, row_spec, col_spec, matrices, turns, first, second, gains, circ_hi, circ_lo,
    yz_pack, yz_in, yz_res, yz_back, col_mid, x_in, x_res, row_mid, x_hi, x_lo,
    yz_send, yz_recv, x_send, x_recv, load_sem,
):
    row, col = lax.axis_index("row"), lax.axis_index("col")
    yz_peers = [
        lax.rem(col // 4 + step[0], 4) * 4 + lax.rem(col % 4 + step[1], 4) for step in YZ_STEPS
    ]
    x_peers = [
        lax.rem(row // 2 + step[0], 4) * 2 + lax.rem(row % 2 + step[1], 2) for step in X_STEPS
    ]

    barrier = pltpu.get_barrier_semaphore()
    for peer in x_peers:
        pl.semaphore_signal(barrier, inc=1, device_id=(peer, col), device_id_type=MESH)
    for peer in yz_peers:
        pl.semaphore_signal(barrier, inc=1, device_id=(row, peer), device_id_type=MESH)

    loads = [
        pltpu.make_async_copy(source, target, load_sem.at[i])
        for i, (source, target) in enumerate([
            (elev_hbm, elev), (row_hbm, row_spec), (first_hbm, first), (second_hbm, second),
            (col_hbm, col_spec), (matrices_hbm, matrices), (turns_hbm, turns),
        ])
    ]
    for load in loads:
        load.start()

    def yz_copies(half, stage, part, source, target, arrived):
        sent, received = yz_send.at[half, stage, part], yz_recv.at[half, stage, part]
        copies = [
            pltpu.make_async_remote_copy(
                src_ref=source(peer), dst_ref=target, send_sem=sent, recv_sem=received,
                device_id=(row, peer), device_id_type=MESH,
            )
            for peer in yz_peers
        ]
        shares = yz_pack.at[half, part].reshape(COL_DEVICES, LINES * HALVES, STRIPS, LANES)
        leaving = shares.at[pl.ds(0, COL_DEVICES - 1)]
        return (
            copies, pltpu.make_async_copy(source(col), target, received),
            pltpu.make_async_copy(arrived, arrived, received), pltpu.make_async_copy(leaving, leaving, sent),
        )

    def x_copies(half, stage, part, band, source, target, arrived, leaving):
        sent, received = x_send.at[half, stage, part, band], x_recv.at[half, stage, part, band]
        copies = [
            pltpu.make_async_remote_copy(
                src_ref=source(peer), dst_ref=target, send_sem=sent, recv_sem=received,
                device_id=(peer, col), device_id_type=MESH,
            )
            for peer in x_peers
        ]
        return (
            copies, pltpu.make_async_copy(source(row), target, received),
            pltpu.make_async_copy(arrived, arrived, received), pltpu.make_async_copy(leaving, leaving, sent),
        )

    def start(exchange):
        for copy in exchange[0] + [exchange[1]]:
            copy.start()

    def wait(exchange):
        exchange[2].wait()

    def wait_sent(exchanges):
        for exchange in exchanges:
            exchange[3].wait()

    def natural(part):
        for line in range(LINES):
            for side in range(HALVES):
                yield line, side, pl.ds(8 * side + LINES * part + line, SIDE, stride=8 * HALVES)

    def banded():
        for turn in range(PARTS):
            for line in range(LINES):
                for side in range(HALVES):
                    where = pl.ds(8 * side + LINES * turn + line, SIDE // PARTS, stride=8 * HALVES)
                    yield turn, line, side, where

    def pack_natural(part):
        rows = elev.reshape(SIDE * 8 * HALVES, LANES)
        for line, side, where in natural(part):
            yz_pack[0, part, :, :, line, side] = rows[where, :].reshape(PAIRS, PARTS, STRIPS, LANES)

    def pack_banded(part):
        rows = row_mid.at[part].reshape(PAIRS * BLOCKS * 8, LANES)
        for turn, line, side, where in banded():
            yz_pack[1, part, :, turn, line, side] = rows[where, :].reshape(PAIRS, STRIPS, LANES)

    def unpack_banded(part):
        rows = col_mid.at[part].reshape(PAIRS * BLOCKS * 8, LANES)
        for turn, line, side, where in banded():
            rows[where, :] = yz_back[0, part, :, turn, line, side].reshape(SIDE // PARTS, LANES)

    def unpack_natural(part):
        rows = out.at[1].reshape(SIDE * 8 * HALVES, LANES)
        for line, side, where in natural(part):
            rows[where, :] = yz_back[1, part, :, :, line, side].reshape(SIDE, LANES)

    def build_circulant(foot):
        real = row_spec[foot, pl.ds(0, 8, stride=2), :]
        imag = row_spec[foot, pl.ds(1, 8, stride=2), :]
        turned_real = jnp.zeros((8, LANES), jnp.float32)
        turned_imag = jnp.zeros((8, LANES), jnp.float32)
        for i in range(8):
            cos, sin = first[0, i], first[1, i]
            turned_real += real[i:i + 1] * cos + imag[i:i + 1] * sin
            turned_imag += imag[i:i + 1] * cos - real[i:i + 1] * sin
        grid = dot_precise(turned_real, second[0]) + dot_precise(turned_imag, second[1])
        index = lax.broadcasted_iota(jnp.int32, (LANES, ROWS), 1)
        group = lax.broadcasted_iota(jnp.int32, (LANES, ROWS), 0)
        spread = dot_precise(grid, jnp.where(index // 8 == group, 1.0, 0.0))
        keep = index[:8] % 8 == group[:8]
        profile = jnp.sum(jnp.where(keep, spread, 0.0), axis=0, keepdims=True)
        rolled = pltpu.roll(jnp.broadcast_to(profile, (LANES, ROWS)), 0, 1, stride=1, stride_axis=0)
        banded_row = lax.broadcasted_iota(jnp.int32, (LANES, LANES), 0)
        natural_row = lax.broadcasted_iota(jnp.int32, (LANES, LANES), 1)
        source = banded_row % 64 // LINES * 8 + banded_row // 64 * LINES + banded_row % LINES
        for target, values in zip((circ_hi, circ_lo), split(rolled)):
            if foot == 1:
                order = jnp.where(source == natural_row, 1.0, 0.0).astype(jnp.bfloat16)
                target[foot] = dot(order, values).astype(jnp.bfloat16)
            else:
                source_column = natural_row % 64 // LINES * 8 + natural_row // 64 * LINES + natural_row % LINES
                order = jnp.where(source_column == banded_row, 1.0, 0.0).astype(jnp.bfloat16)
                for block in range(ROW_DEVICES):
                    lanes = slice(block * LANES, (block + 1) * LANES)
                    target[foot, :, lanes] = dot(values[:, lanes], order).astype(jnp.bfloat16)

    def build_gains(foot):
        for member in range(2):
            for side in range(HALVES):
                values = col_spec[foot, pl.ds(2 * side + member, SIDE, stride=4), :]
                gains[foot, member, side * LANES:(side + 1) * LANES, :] = values.T * (1.0 / (SIDE * SIDE))

    def row_filter(half, part, exchanges):
        foot = 1 - half
        for slot in range(SLOTS):
            lanes = slice(slot * LANES, (slot + 1) * LANES)
            high, low = split(x_in[half, part, :, :, :, slot].reshape(ROWS, LANES))
            for base in (0, ROWS):
                x_hi[base:base + ROWS, lanes] = high
                x_lo[base:base + ROWS, lanes] = low
        for i, owner in enumerate(x_peers + [row]):
            rows = pl.ds(pl.multiple_of(owner * LANES, LANES), ROWS)
            result = dot_split((circ_hi[foot], circ_lo[foot]), (x_hi[rows, :], x_lo[rows, :]))
            for slot in range(SLOTS):
                x_res[half, part, owner, :, :, slot] = result[:, slot * LANES:(slot + 1) * LANES].reshape(
                    PARTS, PAIRS, 8, LANES
                )
            copies = exchanges[0]
            (copies[0] + [copies[1]])[i].start()
        for exchange in exchanges[1:]:
            start(exchange)

    def col_filter(half, part):
        foot = half
        forward = (matrices[0], matrices[1])
        inverse = (matrices[2], matrices[3])
        cos, sin = turns[0], turns[1]
        gain_real, gain_imag = gains[foot, 0], gains[foot, 1]

        def load_line(line):
            return jnp.concatenate(
                [yz_in[half, part, :, :, line, side].reshape(SIDE, LANES) for side in range(HALVES)], 1
            )

        def store_line(line, values):
            for side in range(HALVES):
                yz_res[half, part, :, :, line, side] = values[:, side * LANES:(side + 1) * LANES].reshape(
                    PAIRS, PARTS, STRIPS, LANES
                )

        for line in range(0, LINES, 2):
            field = jnp.concatenate([load_line(line), load_line(line + 1)], 0)
            result = dot_split(forward, split(field))
            real, imag = result[:SIDE], result[SIDE:]
            field = jnp.concatenate([real * cos + imag * sin, imag * cos - real * sin], 1)
            result = dot_split(split(field), inverse)
            real, imag = result[:, :SIDE], result[:, SIDE:]
            field = jnp.concatenate(
                [real * gain_real - imag * gain_imag, real * gain_imag + imag * gain_real], 1
            )
            result = dot_split(split(field), forward)
            real, imag = result[:, :SIDE], result[:, SIDE:]
            field = jnp.concatenate([real * cos - imag * sin, imag * cos + real * sin], 0)
            result = dot_split(inverse, split(field))
            store_line(line, result[:SIDE])
            store_line(line + 1, result[SIDE:])

    def share(owner, part):
        return pl.ds(SLOTS * (PARTS * owner + part), SLOTS)

    def yz_into(half, part):
        return yz_copies(
            half, 0, part, lambda peer: yz_pack.at[half, part, peer // PARTS, peer % PARTS],
            yz_in.at[half, part, col // PARTS, col % PARTS], yz_in.at[half, part],
        )

    def yz_return(half, part):
        return yz_copies(
            half, 1, part, lambda peer: yz_res.at[half, part, peer // PARTS, peer % PARTS],
            yz_back.at[half, part, col // PARTS, col % PARTS], yz_back.at[half, part],
        )

    parts = range(PARTS)
    others = pl.ds(0, ROW_DEVICES - 1)
    half_blocks = pl.ds(0, BLOCKS // PARTS)

    yz_first = [yz_into(0, part) for part in parts]
    x_first = [
        x_copies(
            0, 0, part, 0, lambda peer: elev.at[:, :, share(peer, part)], x_in.at[0, part, row],
            x_in.at[0, part], x_in.at[0, part, others],
        )
        for part in parts
    ]
    loads[0].wait()
    for part in parts:
        pack_natural(part)
    pl.semaphore_wait(barrier, len(YZ_STEPS) + len(X_STEPS))
    for part in parts:
        for copy in interleave(yz_first[part][0], x_first[part][0]):
            copy.start()
        yz_first[part][1].start()
        x_first[part][1].start()
    for load in loads[1:]:
        load.wait()
    for foot in range(2):
        build_circulant(foot)
        build_gains(foot)
    yz_second, x_second = [], []
    for part in parts:
        wait(x_first[part])
        x_second.append([
            x_copies(
                0, 1, part, band, lambda peer: x_res.at[0, part, peer, band],
                row_mid.at[band, :, share(row, part)], row_mid.at[band, :, half_blocks],
                x_res.at[0, part, others, band],
            )
            for band in parts
        ])
        row_filter(0, part, x_second[part])
        wait(yz_first[part])
        col_filter(0, part)
        yz_second.append(yz_return(0, part))
        start(yz_second[part])

    yz_third = [yz_into(1, part) for part in parts]
    x_third = [
        [
            x_copies(
                1, 0, part, band, lambda peer: col_mid.at[band, :, share(peer, part)],
                x_in.at[1, part, row, band], x_in.at[1, part, :, band], x_in.at[1, part, others, band],
            )
            for part in parts
        ]
        for band in parts
    ]

    def x_again(band):
        wait(yz_second[band])
        unpack_banded(band)
        for part in parts:
            start(x_third[band][part])

    def yz_again(band):
        for part in parts:
            wait(x_second[part][band])
        pack_banded(band)
        start(yz_third[band])

    x_again(0)
    yz_again(0)
    yz_again(1)
    x_again(1)
    yz_fourth = [yz_return(1, part) for part in parts]
    x_fourth = [
        x_copies(
            1, 1, part, 0, lambda peer: x_res.at[1, part, peer], out.at[0, :, :, share(row, part)],
            out.at[0, :, :, half_blocks], x_res.at[1, part, others],
        )
        for part in parts
    ]

    def columns_again(part):
        wait(yz_third[part])
        col_filter(1, part)
        start(yz_fourth[part])

    def rows_again(part):
        for band in parts:
            wait(x_third[band][part])
        row_filter(1, part, [x_fourth[part]])

    columns_again(0)
    rows_again(0)
    rows_again(1)
    columns_again(1)
    wait_sent(yz_first + x_first + yz_second + yz_third + sum(x_second + x_third, []))
    for part in parts:
        wait(yz_fourth[part])
        unpack_natural(part)
    for part in parts:
        wait(x_fourth[part])
    wait_sent(yz_fourth + x_fourth)


def finish_kernel(result, out, sems):
    pieces = [
        pltpu.make_async_copy(result.at[foot, band], out.at[foot, band], sems.at[foot, band])
        for foot in range(2)
        for band in range(PARTS)
    ]
    for piece in pieces:
        piece.start()
    for piece in pieces:
        piece.wait()


def body(elevation, row_spectra, col_spectra):
    tiles = elevation.reshape(PARTS, PAIRS, 8, BLOCKS, LANES).transpose(0, 1, 3, 2, 4)
    row_lines = row_spectra.reshape(2, 2, ROWS // LANES, LANES).transpose(0, 2, 1, 3)
    col_lines = col_spectra.reshape(2, 2, SIDE * HALVES, LANES).transpose(0, 2, 1, 3)
    inputs = [
        tiles,
        row_lines.reshape(2, 2 * ROWS // LANES, LANES),
        col_lines.reshape(2, 2 * SIDE * HALVES, LANES),
    ] + [jnp.asarray(table) for table in dft_constants()]
    field = (PARTS, PAIRS, BLOCKS, 8, LANES)
    packed = (PARTS, PAIRS, PARTS, LINES, HALVES, STRIPS, LANES)
    slots = (PARTS, ROW_DEVICES, PARTS, PAIRS, SLOTS, 8, LANES)
    hbm = pl.BlockSpec(memory_space=pltpu.HBM)
    vmem = pl.BlockSpec(memory_space=pltpu.VMEM)
    result = pl.pallas_call(
        kernel,
        out_shape=pltpu.VMEM((2,) + field, jnp.float32),
        in_specs=[hbm] * len(inputs),
        out_specs=vmem,
        scratch_shapes=[pltpu.VMEM(member.shape, member.dtype) for member in inputs] + [
            pltpu.VMEM((2, 2, SIDE, SIDE), jnp.float32),
            pltpu.VMEM((2, LANES, ROWS), jnp.bfloat16),
            pltpu.VMEM((2, LANES, ROWS), jnp.bfloat16),
            pltpu.VMEM((2,) + packed, jnp.float32),
            pltpu.VMEM((2,) + packed, jnp.float32),
            pltpu.VMEM((2,) + packed, jnp.float32),
            pltpu.VMEM((2,) + packed, jnp.float32),
            pltpu.VMEM(field, jnp.float32),
            pltpu.VMEM((2,) + slots, jnp.float32),
            pltpu.VMEM((2,) + slots, jnp.float32),
            pltpu.VMEM(field, jnp.float32),
            pltpu.VMEM((2 * ROWS, SLOTS * LANES), jnp.bfloat16),
            pltpu.VMEM((2 * ROWS, SLOTS * LANES), jnp.bfloat16),
            pltpu.SemaphoreType.DMA((2, 2, PARTS)),
            pltpu.SemaphoreType.DMA((2, 2, PARTS)),
            pltpu.SemaphoreType.DMA((2, 2, PARTS, PARTS)),
            pltpu.SemaphoreType.DMA((2, 2, PARTS, PARTS)),
            pltpu.SemaphoreType.DMA((len(inputs),)),
        ],
        compiler_params=pltpu.CompilerParams(
            collective_id=0, has_side_effects=True, vmem_limit_bytes=52 * 2**20
        ),
    )(*inputs)
    result = pl.pallas_call(
        finish_kernel,
        out_shape=jax.ShapeDtypeStruct((2,) + field, jnp.float32),
        in_specs=[vmem],
        out_specs=pl.BlockSpec(memory_space=pltpu.HBM),
        scratch_shapes=[pltpu.SemaphoreType.DMA((2, PARTS))],
        compiler_params=pltpu.CompilerParams(vmem_limit_bytes=2**20),
    )(result)
    result = result.reshape(2, TILES, BLOCKS, 8, LANES)
    return result.transpose(0, 1, 3, 2, 4).reshape((2,) + elevation.shape)


def solution(mesh):
    in_specs = (P("row", "col"), P(), P())
    out_specs = P(None, "row", "col")
    return jax.shard_map(body, mesh=mesh, in_specs=in_specs, out_specs=out_specs, check_vma=False)
```

```python
import ml_dtypes
import jax
import jax.numpy as jnp
import numpy as np
from jax import lax
from jax.experimental import pallas as pl
from jax.experimental.pallas import tpu as pltpu
from jax.sharding import PartitionSpec as P

MESH = pl.DeviceIdType.MESH
SIDE = 256
LANES = 128
ROW_DEVICES = 8
COL_DEVICES = 16
ROWS = 1024
LOCAL_COLS = 4096
BLOCKS = LOCAL_COLS // LANES
TILES = ROWS // ROW_DEVICES // 8
PARTS = 2
PIECES = 4
SLOTS = BLOCKS // ROW_DEVICES // PARTS
BAND = 8 // PARTS
LINES = 8 // PIECES
HALVES = SIDE // LANES
STRIPS = LOCAL_COLS // SIDE
PAIRS = TILES // PARTS
YZ_STEPS = [
    (1, 1), (3, 3), (2, 2), (1, 3), (3, 1), (2, 1), (1, 2), (2, 3),
    (3, 2), (2, 0), (0, 2), (1, 0), (0, 1), (3, 0), (0, 3),
]
X_STEPS = [(1, 0), (3, 0), (1, 1), (3, 1), (2, 0), (2, 1), (0, 1)]


def split_constant(values):
    high = values.astype(ml_dtypes.bfloat16)
    low = (values - high.astype(np.float64)).astype(ml_dtypes.bfloat16)
    return [high, low]


def dft_constants():
    index = np.arange(SIDE)
    angles = 2.0 * np.pi / SIDE * (np.outer(index, index) % SIDE)
    cos, sin = np.cos(angles), np.sin(angles)
    forward = np.block([[cos, sin], [-sin, cos]])
    inverse = np.block([[cos, -sin], [sin, cos]])
    matrices = np.stack(split_constant(forward) + split_constant(inverse))
    turn = 2.0 * np.pi / (SIDE * SIDE) * np.outer(index, index)
    turns = np.stack([np.cos(turn), np.sin(turn)]).astype(np.float32)
    low = np.arange(8)
    lane = np.arange(LANES)
    first = 2.0 * np.pi / ROWS * (
        low[None, :, None] * (LANES * low[:, None, None] + lane[None, None, :]) % ROWS
    )
    first = np.stack([np.cos(first), np.sin(first)]).astype(np.float32)
    second = 2.0 * np.pi / LANES * (np.outer(lane, lane) % LANES)
    second = (np.stack([np.cos(second), np.sin(second)]) / ROWS).astype(np.float32)
    return matrices, turns, first, second


def split(values):
    high = values.astype(jnp.bfloat16)
    low = (values - high.astype(jnp.float32)).astype(jnp.bfloat16)
    return high, low


def dot(left, right):
    return jnp.dot(left, right, preferred_element_type=jnp.float32)


def dot_precise(left, right):
    return jnp.dot(
        left, right, preferred_element_type=jnp.float32, precision=lax.Precision.HIGHEST
    )


def dot_split(left, right):
    return dot(left[0], right[0]) + (dot(left[1], right[0]) + dot(left[0], right[1]))


def interleave(first, second):
    merged = []
    count = max(len(first), len(second))
    for i in range(count):
        for member in (first, second):
            merged += member[len(member) * i // count:len(member) * (i + 1) // count]
    return merged


def kernel(
    elev_hbm, row_hbm, col_hbm, matrices_hbm, turns_hbm, first_hbm, second_hbm,
    out,
    elev, row_spec, col_spec, matrices, turns, first, second, gains, circ_hi, circ_lo,
    yz_pack, yz_in, yz_res, yz_back, col_mid, x_in, x_res, row_mid, x_hi, x_lo,
    yz_send, yz_recv, x_send, x_recv, load_sem,
):
    row, col = lax.axis_index("row"), lax.axis_index("col")
    yz_peers = [
        lax.rem(col // 4 + step[0], 4) * 4 + lax.rem(col % 4 + step[1], 4) for step in YZ_STEPS
    ]
    x_peers = [
        lax.rem(row // 2 + step[0], 4) * 2 + lax.rem(row % 2 + step[1], 2) for step in X_STEPS
    ]

    barrier = pltpu.get_barrier_semaphore()
    for peer in x_peers:
        pl.semaphore_signal(barrier, inc=1, device_id=(peer, col), device_id_type=MESH)
    for peer in yz_peers:
        pl.semaphore_signal(barrier, inc=1, device_id=(row, peer), device_id_type=MESH)

    loads = [
        pltpu.make_async_copy(source, target, load_sem.at[i])
        for i, (source, target) in enumerate([
            (elev_hbm, elev), (row_hbm, row_spec), (first_hbm, first), (second_hbm, second),
            (col_hbm, col_spec), (matrices_hbm, matrices), (turns_hbm, turns),
        ])
    ]
    for load in loads:
        load.start()

    def yz_copies(half, stage, piece, source, target, arrived):
        sent, received = yz_send.at[half, stage, piece], yz_recv.at[half, stage, piece]
        copies = [
            pltpu.make_async_remote_copy(
                src_ref=source(peer), dst_ref=target, send_sem=sent, recv_sem=received,
                device_id=(row, peer), device_id_type=MESH,
            )
            for peer in yz_peers
        ]
        shares = yz_pack.at[half, piece].reshape(COL_DEVICES, LINES * HALVES, STRIPS, LANES)
        leaving = shares.at[pl.ds(0, COL_DEVICES - 1)]
        return (
            copies, pltpu.make_async_copy(source(col), target, received),
            pltpu.make_async_copy(arrived, arrived, received), pltpu.make_async_copy(leaving, leaving, sent),
        )

    def x_copies(half, stage, part, band, source, target, arrived, leaving):
        sent, received = x_send.at[half, stage, part, band], x_recv.at[half, stage, part, band]
        copies = [
            pltpu.make_async_remote_copy(
                src_ref=source(peer), dst_ref=target, send_sem=sent, recv_sem=received,
                device_id=(peer, col), device_id_type=MESH,
            )
            for peer in x_peers
        ]
        return (
            copies, pltpu.make_async_copy(source(row), target, received),
            pltpu.make_async_copy(arrived, arrived, received), pltpu.make_async_copy(leaving, leaving, sent),
        )

    def start(exchange):
        for copy in exchange[0] + [exchange[1]]:
            copy.start()

    def wait(exchange):
        exchange[2].wait()

    def wait_sent(exchanges):
        for exchange in exchanges:
            exchange[3].wait()

    def natural(piece):
        for line in range(LINES):
            for side in range(HALVES):
                yield line, side, pl.ds(8 * side + LINES * piece + line, SIDE, stride=8 * HALVES)

    def banded(piece):
        begin = LINES * piece % BAND
        for turn in range(PARTS):
            for line in range(LINES):
                for side in range(HALVES):
                    where = pl.ds(8 * side + BAND * turn + begin + line, SIDE // PARTS, stride=8 * HALVES)
                    yield turn, line, side, where

    def pack_natural(piece):
        rows = elev.reshape(SIDE * 8 * HALVES, LANES)
        for line, side, where in natural(piece):
            yz_pack[0, piece, :, :, line, side] = rows[where, :].reshape(PAIRS, PARTS, STRIPS, LANES)

    def pack_banded(piece):
        rows = row_mid.at[LINES * piece // BAND].reshape(PAIRS * BLOCKS * 8, LANES)
        for turn, line, side, where in banded(piece):
            yz_pack[1, piece, :, turn, line, side] = rows[where, :].reshape(PAIRS, STRIPS, LANES)

    def unpack_banded(piece):
        rows = col_mid.at[LINES * piece // BAND].reshape(PAIRS * BLOCKS * 8, LANES)
        for turn, line, side, where in banded(piece):
            rows[where, :] = yz_back[0, piece, :, turn, line, side].reshape(SIDE // PARTS, LANES)

    def unpack_natural(piece):
        rows = out.at[1].reshape(SIDE * 8 * HALVES, LANES)
        for line, side, where in natural(piece):
            rows[where, :] = yz_back[1, piece, :, :, line, side].reshape(SIDE, LANES)

    def build_circulant(foot):
        real = row_spec[foot, pl.ds(0, 8, stride=2), :]
        imag = row_spec[foot, pl.ds(1, 8, stride=2), :]
        turned_real = jnp.zeros((8, LANES), jnp.float32)
        turned_imag = jnp.zeros((8, LANES), jnp.float32)
        for i in range(8):
            cos, sin = first[0, i], first[1, i]
            turned_real += real[i:i + 1] * cos + imag[i:i + 1] * sin
            turned_imag += imag[i:i + 1] * cos - real[i:i + 1] * sin
        grid = dot_precise(turned_real, second[0]) + dot_precise(turned_imag, second[1])
        index = lax.broadcasted_iota(jnp.int32, (LANES, ROWS), 1)
        group = lax.broadcasted_iota(jnp.int32, (LANES, ROWS), 0)
        spread = dot_precise(grid, jnp.where(index // 8 == group, 1.0, 0.0))
        keep = index[:8] % 8 == group[:8]
        profile = jnp.sum(jnp.where(keep, spread, 0.0), axis=0, keepdims=True)
        rolled = pltpu.roll(jnp.broadcast_to(profile, (LANES, ROWS)), 0, 1, stride=1, stride_axis=0)
        banded_row = lax.broadcasted_iota(jnp.int32, (LANES, LANES), 0)
        natural_row = lax.broadcasted_iota(jnp.int32, (LANES, LANES), 1)
        source = banded_row % 64 // BAND * 8 + banded_row // 64 * BAND + banded_row % BAND
        for target, values in zip((circ_hi, circ_lo), split(rolled)):
            if foot == 1:
                order = jnp.where(source == natural_row, 1.0, 0.0).astype(jnp.bfloat16)
                target[foot] = dot(order, values).astype(jnp.bfloat16)
            else:
                source_column = natural_row % 64 // BAND * 8 + natural_row // 64 * BAND + natural_row % BAND
                order = jnp.where(source_column == banded_row, 1.0, 0.0).astype(jnp.bfloat16)
                for block in range(ROW_DEVICES):
                    lanes = slice(block * LANES, (block + 1) * LANES)
                    target[foot, :, lanes] = dot(values[:, lanes], order).astype(jnp.bfloat16)

    def build_gains(foot):
        for member in range(2):
            for side in range(HALVES):
                values = col_spec[foot, pl.ds(2 * side + member, SIDE, stride=4), :]
                gains[foot, member, side * LANES:(side + 1) * LANES, :] = values.T * (1.0 / (SIDE * SIDE))

    def row_filter(half, part, exchanges):
        foot = 1 - half
        for slot in range(SLOTS):
            lanes = slice(slot * LANES, (slot + 1) * LANES)
            high, low = split(x_in[half, part, :, :, :, slot].reshape(ROWS, LANES))
            for base in (0, ROWS):
                x_hi[base:base + ROWS, lanes] = high
                x_lo[base:base + ROWS, lanes] = low
        for i, owner in enumerate(x_peers + [row]):
            rows = pl.ds(pl.multiple_of(owner * LANES, LANES), ROWS)
            result = dot_split((circ_hi[foot], circ_lo[foot]), (x_hi[rows, :], x_lo[rows, :]))
            for slot in range(SLOTS):
                x_res[half, part, owner, :, :, slot] = result[:, slot * LANES:(slot + 1) * LANES].reshape(
                    PARTS, PAIRS, 8, LANES
                )
            copies = exchanges[0]
            (copies[0] + [copies[1]])[i].start()
        for exchange in exchanges[1:]:
            start(exchange)

    def col_filter(half, piece):
        foot = half
        forward = (matrices[0], matrices[1])
        inverse = (matrices[2], matrices[3])
        cos, sin = turns[0], turns[1]
        gain_real, gain_imag = gains[foot, 0], gains[foot, 1]

        def load_line(line):
            return jnp.concatenate(
                [yz_in[half, piece, :, :, line, side].reshape(SIDE, LANES) for side in range(HALVES)], 1
            )

        def store_line(line, values):
            for side in range(HALVES):
                yz_res[half, piece, :, :, line, side] = values[:, side * LANES:(side + 1) * LANES].reshape(
                    PAIRS, PARTS, STRIPS, LANES
                )

        for line in range(0, LINES, 2):
            field = jnp.concatenate([load_line(line), load_line(line + 1)], 0)
            result = dot_split(forward, split(field))
            real, imag = result[:SIDE], result[SIDE:]
            field = jnp.concatenate([real * cos + imag * sin, imag * cos - real * sin], 1)
            result = dot_split(split(field), inverse)
            real, imag = result[:, :SIDE], result[:, SIDE:]
            field = jnp.concatenate(
                [real * gain_real - imag * gain_imag, real * gain_imag + imag * gain_real], 1
            )
            result = dot_split(split(field), forward)
            real, imag = result[:, :SIDE], result[:, SIDE:]
            field = jnp.concatenate([real * cos - imag * sin, imag * cos + real * sin], 0)
            result = dot_split(inverse, split(field))
            store_line(line, result[:SIDE])
            store_line(line + 1, result[SIDE:])

    def share(owner, part):
        return pl.ds(SLOTS * (PARTS * owner + part), SLOTS)

    def yz_into(half, piece):
        return yz_copies(
            half, 0, piece, lambda peer: yz_pack.at[half, piece, peer // PARTS, peer % PARTS],
            yz_in.at[half, piece, col // PARTS, col % PARTS], yz_in.at[half, piece],
        )

    def yz_return(half, piece):
        return yz_copies(
            half, 1, piece, lambda peer: yz_res.at[half, piece, peer // PARTS, peer % PARTS],
            yz_back.at[half, piece, col // PARTS, col % PARTS], yz_back.at[half, piece],
        )

    parts = range(PARTS)
    pieces = range(PIECES)
    others = pl.ds(0, ROW_DEVICES - 1)
    half_blocks = pl.ds(0, BLOCKS // PARTS)

    yz_first = [yz_into(0, piece) for piece in pieces]
    x_first = [
        x_copies(
            0, 0, part, 0, lambda peer: elev.at[:, :, share(peer, part)], x_in.at[0, part, row],
            x_in.at[0, part], x_in.at[0, part, others],
        )
        for part in parts
    ]
    loads[0].wait()
    for piece in pieces[:2]:
        pack_natural(piece)
    pl.semaphore_wait(barrier, len(YZ_STEPS) + len(X_STEPS))
    for part in parts:
        members = yz_first[2 * part:2 * part + 2]
        for copy in interleave(members[0][0] + members[1][0], x_first[part][0]):
            copy.start()
        for exchange in members + [x_first[part]]:
            exchange[1].start()
        if part == 0:
            for piece in pieces[2:]:
                pack_natural(piece)
    for load in loads[1:]:
        load.wait()
    for foot in range(2):
        build_circulant(foot)
        build_gains(foot)
    yz_second = [yz_return(0, piece) for piece in pieces]
    x_second = [
        [
            x_copies(
                0, 1, part, band, lambda peer: x_res.at[0, part, peer, band],
                row_mid.at[band, :, share(row, part)], row_mid.at[band, :, half_blocks],
                x_res.at[0, part, others, band],
            )
            for band in parts
        ]
        for part in parts
    ]

    def rows_once(part):
        wait(x_first[part])
        row_filter(0, part, x_second[part])

    def columns_once(piece):
        wait(yz_first[piece])
        col_filter(0, piece)
        start(yz_second[piece])

    columns_once(0)
    rows_once(0)
    columns_once(1)
    columns_once(2)
    rows_once(1)
    columns_once(3)

    yz_third = [yz_into(1, piece) for piece in pieces]
    x_third = [
        [
            x_copies(
                1, 0, part, band, lambda peer: col_mid.at[band, :, share(peer, part)],
                x_in.at[1, part, row, band], x_in.at[1, part, :, band], x_in.at[1, part, others, band],
            )
            for part in parts
        ]
        for band in parts
    ]

    def x_again(band):
        for piece in pieces[2 * band:2 * band + 2]:
            wait(yz_second[piece])
            unpack_banded(piece)
        for part in parts:
            start(x_third[band][part])

    def yz_again(band):
        for part in parts:
            wait(x_second[part][band])
        for piece in pieces[2 * band:2 * band + 2]:
            pack_banded(piece)
            start(yz_third[piece])

    x_again(0)
    yz_again(0)
    yz_again(1)
    x_again(1)
    yz_fourth = [yz_return(1, piece) for piece in pieces]
    x_fourth = [
        x_copies(
            1, 1, part, 0, lambda peer: x_res.at[1, part, peer], out.at[0, :, :, share(row, part)],
            out.at[0, :, :, half_blocks], x_res.at[1, part, others],
        )
        for part in parts
    ]

    def columns_again(piece):
        wait(yz_third[piece])
        col_filter(1, piece)
        start(yz_fourth[piece])

    def rows_again(part):
        for band in parts:
            wait(x_third[band][part])
        row_filter(1, part, [x_fourth[part]])

    columns_again(0)
    columns_again(1)
    rows_again(0)
    columns_again(2)
    rows_again(1)
    columns_again(3)
    wait_sent(yz_first + x_first + yz_second + yz_third + sum(x_second + x_third, []))
    for piece in pieces:
        wait(yz_fourth[piece])
        unpack_natural(piece)
    for part in parts:
        wait(x_fourth[part])
    wait_sent(yz_fourth + x_fourth)


def finish_kernel(result, out, sems):
    pieces = [
        pltpu.make_async_copy(result.at[foot, band], out.at[foot, band], sems.at[foot, band])
        for foot in range(2)
        for band in range(PARTS)
    ]
    for piece in pieces:
        piece.start()
    for piece in pieces:
        piece.wait()


def body(elevation, row_spectra, col_spectra):
    tiles = elevation.reshape(PARTS, PAIRS, 8, BLOCKS, LANES).transpose(0, 1, 3, 2, 4)
    row_lines = row_spectra.reshape(2, 2, ROWS // LANES, LANES).transpose(0, 2, 1, 3)
    col_lines = col_spectra.reshape(2, 2, SIDE * HALVES, LANES).transpose(0, 2, 1, 3)
    inputs = [
        tiles,
        row_lines.reshape(2, 2 * ROWS // LANES, LANES),
        col_lines.reshape(2, 2 * SIDE * HALVES, LANES),
    ] + [jnp.asarray(table) for table in dft_constants()]
    field = (PARTS, PAIRS, BLOCKS, 8, LANES)
    packed = (PIECES, PAIRS, PARTS, LINES, HALVES, STRIPS, LANES)
    slots = (PARTS, ROW_DEVICES, PARTS, PAIRS, SLOTS, 8, LANES)
    hbm = pl.BlockSpec(memory_space=pltpu.HBM)
    vmem = pl.BlockSpec(memory_space=pltpu.VMEM)
    result = pl.pallas_call(
        kernel,
        out_shape=pltpu.VMEM((2,) + field, jnp.float32),
        in_specs=[hbm] * len(inputs),
        out_specs=vmem,
        scratch_shapes=[pltpu.VMEM(member.shape, member.dtype) for member in inputs] + [
            pltpu.VMEM((2, 2, SIDE, SIDE), jnp.float32),
            pltpu.VMEM((2, LANES, ROWS), jnp.bfloat16),
            pltpu.VMEM((2, LANES, ROWS), jnp.bfloat16),
            pltpu.VMEM((2,) + packed, jnp.float32),
            pltpu.VMEM((2,) + packed, jnp.float32),
            pltpu.VMEM((2,) + packed, jnp.float32),
            pltpu.VMEM((2,) + packed, jnp.float32),
            pltpu.VMEM(field, jnp.float32),
            pltpu.VMEM((2,) + slots, jnp.float32),
            pltpu.VMEM((2,) + slots, jnp.float32),
            pltpu.VMEM(field, jnp.float32),
            pltpu.VMEM((2 * ROWS, SLOTS * LANES), jnp.bfloat16),
            pltpu.VMEM((2 * ROWS, SLOTS * LANES), jnp.bfloat16),
            pltpu.SemaphoreType.DMA((2, 2, PIECES)),
            pltpu.SemaphoreType.DMA((2, 2, PIECES)),
            pltpu.SemaphoreType.DMA((2, 2, PARTS, PARTS)),
            pltpu.SemaphoreType.DMA((2, 2, PARTS, PARTS)),
            pltpu.SemaphoreType.DMA((len(inputs),)),
        ],
        compiler_params=pltpu.CompilerParams(
            collective_id=0, has_side_effects=True, vmem_limit_bytes=52 * 2**20
        ),
    )(*inputs)
    result = pl.pallas_call(
        finish_kernel,
        out_shape=jax.ShapeDtypeStruct((2,) + field, jnp.float32),
        in_specs=[vmem],
        out_specs=pl.BlockSpec(memory_space=pltpu.HBM),
        scratch_shapes=[pltpu.SemaphoreType.DMA((2, PARTS))],
        compiler_params=pltpu.CompilerParams(vmem_limit_bytes=2**20),
    )(result)
    result = result.reshape(2, TILES, BLOCKS, 8, LANES)
    return result.transpose(0, 1, 3, 2, 4).reshape((2,) + elevation.shape)


def solution(mesh):
    in_specs = (P("row", "col"), P(), P())
    out_specs = P(None, "row", "col")
    return jax.shard_map(body, mesh=mesh, in_specs=in_specs, out_specs=out_specs, check_vma=False)
```

```python
import ml_dtypes
import jax
import jax.numpy as jnp
import numpy as np
from jax import lax
from jax.experimental import pallas as pl
from jax.experimental.pallas import tpu as pltpu
from jax.sharding import PartitionSpec as P

MESH = pl.DeviceIdType.MESH
SIDE = 256
LANES = 128
ROW_DEVICES = 8
COL_DEVICES = 16
ROWS = 1024
LOCAL_COLS = 4096
BLOCKS = LOCAL_COLS // LANES
TILES = ROWS // ROW_DEVICES // 8
PARTS = 2
PIECES = 4
SLOTS = BLOCKS // ROW_DEVICES // PARTS
BAND = 8 // PARTS
LINES = 8 // PIECES
HALVES = SIDE // LANES
STRIPS = LOCAL_COLS // SIDE
PAIRS = TILES // PARTS
X_CUTS = 1
GROUPS = [[(0,), (1,), (2,), (3,)]] * 4
FIRST_ORDER = ["c0", "r0", "c1", "c2", "r1", "c3"]
SECOND_ORDER = ["c0", "c1", "r0", "c2", "r1", "c3"]
YZ_STEPS = [
    (1, 1), (3, 3), (2, 2), (1, 3), (3, 1), (2, 1), (1, 2), (2, 3),
    (3, 2), (2, 0), (0, 2), (1, 0), (0, 1), (3, 0), (0, 3),
]
X_STEPS = [(1, 0), (3, 0), (1, 1), (3, 1), (2, 0), (2, 1), (0, 1)]


def split_constant(values):
    high = values.astype(ml_dtypes.bfloat16)
    low = (values - high.astype(np.float64)).astype(ml_dtypes.bfloat16)
    return [high, low]


def dft_constants():
    index = np.arange(SIDE)
    angles = 2.0 * np.pi / SIDE * (np.outer(index, index) % SIDE)
    cos, sin = np.cos(angles), np.sin(angles)
    forward = np.block([[cos, sin], [-sin, cos]])
    inverse = np.block([[cos, -sin], [sin, cos]])
    matrices = np.stack(split_constant(forward) + split_constant(inverse))
    turn = 2.0 * np.pi / (SIDE * SIDE) * np.outer(index, index)
    turns = np.stack([np.cos(turn), np.sin(turn)]).astype(np.float32)
    low = np.arange(8)
    lane = np.arange(LANES)
    first = 2.0 * np.pi / ROWS * (
        low[None, :, None] * (LANES * low[:, None, None] + lane[None, None, :]) % ROWS
    )
    first = np.stack([np.cos(first), np.sin(first)]).astype(np.float32)
    second = 2.0 * np.pi / LANES * (np.outer(lane, lane) % LANES)
    second = (np.stack([np.cos(second), np.sin(second)]) / ROWS).astype(np.float32)
    return matrices, turns, first, second


def split(values):
    high = values.astype(jnp.bfloat16)
    low = (values - high.astype(jnp.float32)).astype(jnp.bfloat16)
    return high, low


def dot(left, right):
    return jnp.dot(left, right, preferred_element_type=jnp.float32)


def dot_precise(left, right):
    return jnp.dot(
        left, right, preferred_element_type=jnp.float32, precision=lax.Precision.HIGHEST
    )


def dot_split(left, right):
    return dot(left[0], right[0]) + (dot(left[1], right[0]) + dot(left[0], right[1]))


def interleave(first, second):
    merged = []
    count = max(len(first), len(second))
    for i in range(count):
        for member in (first, second):
            merged += member[len(member) * i // count:len(member) * (i + 1) // count]
    return merged


def kernel(
    elev_hbm, row_hbm, col_hbm, matrices_hbm, turns_hbm, first_hbm, second_hbm,
    out,
    elev, row_spec, col_spec, matrices, turns, first, second, gains, circ_hi, circ_lo,
    yz_pack, yz_in, yz_res, yz_back, col_mid, x_in, x_res, row_mid, x_hi, x_lo,
    yz_send, yz_recv, x_send, x_recv, load_sem,
):
    row, col = lax.axis_index("row"), lax.axis_index("col")
    yz_peers = [
        lax.rem(col // 4 + step[0], 4) * 4 + lax.rem(col % 4 + step[1], 4) for step in YZ_STEPS
    ]
    x_peers = [
        lax.rem(row // 2 + step[0], 4) * 2 + lax.rem(row % 2 + step[1], 2) for step in X_STEPS
    ]

    barrier = pltpu.get_barrier_semaphore()
    for peer in x_peers:
        pl.semaphore_signal(barrier, inc=1, device_id=(peer, col), device_id_type=MESH)
    for peer in yz_peers:
        pl.semaphore_signal(barrier, inc=1, device_id=(row, peer), device_id_type=MESH)

    loads = [
        pltpu.make_async_copy(source, target, load_sem.at[i])
        for i, (source, target) in enumerate([
            (elev_hbm, elev), (row_hbm, row_spec), (first_hbm, first), (second_hbm, second),
            (col_hbm, col_spec), (matrices_hbm, matrices), (turns_hbm, turns),
        ])
    ]
    for load in loads:
        load.start()

    def yz_copies(half, stage, group, source, target):
        sent, received = yz_send.at[half, stage, group[0]], yz_recv.at[half, stage, group[0]]
        count = len(group)
        pieces = pl.ds(group[0], count)

        def piece_of(field, peer):
            return field.at[half, pieces, peer // PARTS, peer % PARTS]

        copies = [
            pltpu.make_async_remote_copy(
                src_ref=piece_of(source, peer), dst_ref=piece_of(target, col), send_sem=sent,
                recv_sem=received, device_id=(row, peer), device_id_type=MESH,
            )
            for peer in yz_peers
        ]
        arrived = target.at[half, pieces]
        shares = source.at[half, pieces].reshape(count * COL_DEVICES, LINES * HALVES, STRIPS, LANES)
        leaving = shares.at[pl.ds(0, count * (COL_DEVICES - 1))]
        return (
            copies, pltpu.make_async_copy(piece_of(source, col), piece_of(target, col), received),
            pltpu.make_async_copy(arrived, arrived, received), pltpu.make_async_copy(leaving, leaving, sent),
        )

    def x_copies(half, stage, part, band, source, target, arrived, leaving):
        sent, received = x_send.at[half, stage, part, band], x_recv.at[half, stage, part, band]
        cuts = [pl.ds(cut * PAIRS // X_CUTS, PAIRS // X_CUTS) for cut in range(X_CUTS)]
        copies = [
            pltpu.make_async_remote_copy(
                src_ref=source(peer).at[cut], dst_ref=target.at[cut], send_sem=sent, recv_sem=received,
                device_id=(peer, col), device_id_type=MESH,
            )
            for peer in x_peers
            for cut in cuts
        ]
        return (
            copies, pltpu.make_async_copy(source(row), target, received),
            pltpu.make_async_copy(arrived, arrived, received), pltpu.make_async_copy(leaving, leaving, sent),
        )

    def start(exchange):
        for copy in exchange[0] + [exchange[1]]:
            copy.start()

    def wait(exchange):
        exchange[2].wait()

    def wait_sent(exchanges):
        for exchange in exchanges:
            exchange[3].wait()

    def natural(piece):
        for line in range(LINES):
            for side in range(HALVES):
                yield line, side, pl.ds(8 * side + LINES * piece + line, SIDE, stride=8 * HALVES)

    def banded(piece):
        begin = LINES * piece % BAND
        for turn in range(PARTS):
            for line in range(LINES):
                for side in range(HALVES):
                    where = pl.ds(8 * side + BAND * turn + begin + line, SIDE // PARTS, stride=8 * HALVES)
                    yield turn, line, side, where

    def pack_natural(piece):
        rows = elev.reshape(SIDE * 8 * HALVES, LANES)
        for line, side, where in natural(piece):
            yz_pack[0, piece, :, :, line, side] = rows[where, :].reshape(PAIRS, PARTS, STRIPS, LANES)

    def pack_banded(piece):
        rows = row_mid.at[LINES * piece // BAND].reshape(PAIRS * BLOCKS * 8, LANES)
        for turn, line, side, where in banded(piece):
            yz_pack[1, piece, :, turn, line, side] = rows[where, :].reshape(PAIRS, STRIPS, LANES)

    def unpack_banded(piece):
        rows = col_mid.at[LINES * piece // BAND].reshape(PAIRS * BLOCKS * 8, LANES)
        for turn, line, side, where in banded(piece):
            rows[where, :] = yz_back[0, piece, :, turn, line, side].reshape(SIDE // PARTS, LANES)

    def unpack_natural(piece):
        rows = out.at[1].reshape(SIDE * 8 * HALVES, LANES)
        for line, side, where in natural(piece):
            rows[where, :] = yz_back[1, piece, :, :, line, side].reshape(SIDE, LANES)

    def build_circulant(foot):
        real = row_spec[foot, pl.ds(0, 8, stride=2), :]
        imag = row_spec[foot, pl.ds(1, 8, stride=2), :]
        turned_real = jnp.zeros((8, LANES), jnp.float32)
        turned_imag = jnp.zeros((8, LANES), jnp.float32)
        for i in range(8):
            cos, sin = first[0, i], first[1, i]
            turned_real += real[i:i + 1] * cos + imag[i:i + 1] * sin
            turned_imag += imag[i:i + 1] * cos - real[i:i + 1] * sin
        grid = dot_precise(turned_real, second[0]) + dot_precise(turned_imag, second[1])
        index = lax.broadcasted_iota(jnp.int32, (LANES, ROWS), 1)
        group = lax.broadcasted_iota(jnp.int32, (LANES, ROWS), 0)
        spread = dot_precise(grid, jnp.where(index // 8 == group, 1.0, 0.0))
        keep = index[:8] % 8 == group[:8]
        profile = jnp.sum(jnp.where(keep, spread, 0.0), axis=0, keepdims=True)
        rolled = pltpu.roll(jnp.broadcast_to(profile, (LANES, ROWS)), 0, 1, stride=1, stride_axis=0)
        banded_row = lax.broadcasted_iota(jnp.int32, (LANES, LANES), 0)
        natural_row = lax.broadcasted_iota(jnp.int32, (LANES, LANES), 1)
        source = banded_row % 64 // BAND * 8 + banded_row // 64 * BAND + banded_row % BAND
        for target, values in zip((circ_hi, circ_lo), split(rolled)):
            if foot == 1:
                order = jnp.where(source == natural_row, 1.0, 0.0).astype(jnp.bfloat16)
                target[foot] = dot(order, values).astype(jnp.bfloat16)
            else:
                source_column = natural_row % 64 // BAND * 8 + natural_row // 64 * BAND + natural_row % BAND
                order = jnp.where(source_column == banded_row, 1.0, 0.0).astype(jnp.bfloat16)
                for block in range(ROW_DEVICES):
                    lanes = slice(block * LANES, (block + 1) * LANES)
                    target[foot, :, lanes] = dot(values[:, lanes], order).astype(jnp.bfloat16)

    def build_gains(foot):
        for member in range(2):
            for side in range(HALVES):
                values = col_spec[foot, pl.ds(2 * side + member, SIDE, stride=4), :]
                gains[foot, member, side * LANES:(side + 1) * LANES, :] = values.T * (1.0 / (SIDE * SIDE))

    def row_filter(half, part, exchanges):
        foot = 1 - half
        for slot in range(SLOTS):
            lanes = slice(slot * LANES, (slot + 1) * LANES)
            high, low = split(x_in[half, part, :, :, :, slot].reshape(ROWS, LANES))
            for base in (0, ROWS):
                x_hi[base:base + ROWS, lanes] = high
                x_lo[base:base + ROWS, lanes] = low
        for i, owner in enumerate(x_peers + [row]):
            rows = pl.ds(pl.multiple_of(owner * LANES, LANES), ROWS)
            result = dot_split((circ_hi[foot], circ_lo[foot]), (x_hi[rows, :], x_lo[rows, :]))
            for slot in range(SLOTS):
                x_res[half, part, owner, :, :, slot] = result[:, slot * LANES:(slot + 1) * LANES].reshape(
                    PARTS, PAIRS, 8, LANES
                )
            copies = exchanges[0][0][i * X_CUTS:(i + 1) * X_CUTS]
            for copy in copies if i < len(x_peers) else [exchanges[0][1]]:
                copy.start()
        for exchange in exchanges[1:]:
            start(exchange)

    def col_filter(half, piece):
        foot = half
        forward = (matrices[0], matrices[1])
        inverse = (matrices[2], matrices[3])
        cos, sin = turns[0], turns[1]
        gain_real, gain_imag = gains[foot, 0], gains[foot, 1]

        def load_line(line):
            return jnp.concatenate(
                [yz_in[half, piece, :, :, line, side].reshape(SIDE, LANES) for side in range(HALVES)], 1
            )

        def store_line(line, values):
            for side in range(HALVES):
                yz_res[half, piece, :, :, line, side] = values[:, side * LANES:(side + 1) * LANES].reshape(
                    PAIRS, PARTS, STRIPS, LANES
                )

        for line in range(0, LINES, 2):
            field = jnp.concatenate([load_line(line), load_line(line + 1)], 0)
            result = dot_split(forward, split(field))
            real, imag = result[:SIDE], result[SIDE:]
            field = jnp.concatenate([real * cos + imag * sin, imag * cos - real * sin], 1)
            result = dot_split(split(field), inverse)
            real, imag = result[:, :SIDE], result[:, SIDE:]
            field = jnp.concatenate(
                [real * gain_real - imag * gain_imag, real * gain_imag + imag * gain_real], 1
            )
            result = dot_split(split(field), forward)
            real, imag = result[:, :SIDE], result[:, SIDE:]
            field = jnp.concatenate([real * cos - imag * sin, imag * cos + real * sin], 0)
            result = dot_split(inverse, split(field))
            store_line(line, result[:SIDE])
            store_line(line + 1, result[SIDE:])

    def share(owner, part):
        return pl.ds(SLOTS * (PARTS * owner + part), SLOTS)

    def yz_exchange(half, stage):
        source, target = ((yz_pack, yz_in), (yz_res, yz_back))[stage]
        return {group: yz_copies(half, stage, group, source, target) for group in GROUPS[2 * half + stage]}

    def wait_piece(exchange, piece):
        for group in exchange:
            if group[0] == piece:
                wait(exchange[group])

    def start_piece(exchange, piece):
        for group in exchange:
            if group[-1] == piece:
                start(exchange[group])

    parts = range(PARTS)
    pieces = range(PIECES)
    others = pl.ds(0, ROW_DEVICES - 1)
    half_blocks = pl.ds(0, BLOCKS // PARTS)

    yz_first = yz_exchange(0, 0)
    x_first = [
        [
            x_copies(
                0, 0, part, band, lambda peer: elev.at[band, :, share(peer, part)],
                x_in.at[0, part, row, band], x_in.at[0, part, :, band], x_in.at[0, part, others, band],
            )
            for band in parts
        ]
        for part in parts
    ]
    loads[0].wait()
    for piece in pieces[:2]:
        pack_natural(piece)
    pl.semaphore_wait(barrier, len(YZ_STEPS) + len(X_STEPS))
    for part in parts:
        members = [yz_first[group] for group in yz_first if group[0] // 2 == part]
        for copy in interleave(
            sum((member[0] for member in members), []), x_first[part][0][0] + x_first[part][1][0]
        ):
            copy.start()
        for exchange in members + x_first[part]:
            exchange[1].start()
        if part == 0:
            for piece in pieces[2:]:
                pack_natural(piece)
    for load in loads[1:]:
        load.wait()
    for foot in range(2):
        build_circulant(foot)
        build_gains(foot)
    yz_second = yz_exchange(0, 1)
    x_second = [
        [
            x_copies(
                0, 1, part, band, lambda peer: x_res.at[0, part, peer, band],
                row_mid.at[band, :, share(row, part)], row_mid.at[band, :, half_blocks],
                x_res.at[0, part, others, band],
            )
            for band in parts
        ]
        for part in parts
    ]

    def rows_once(part):
        for band in parts:
            wait(x_first[part][band])
        row_filter(0, part, x_second[part])

    def columns_once(piece):
        wait_piece(yz_first, piece)
        col_filter(0, piece)
        start_piece(yz_second, piece)

    for step in FIRST_ORDER:
        (columns_once if step[0] == "c" else rows_once)(int(step[1]))

    yz_third = yz_exchange(1, 0)
    x_third = [
        [
            x_copies(
                1, 0, part, band, lambda peer: col_mid.at[band, :, share(peer, part)],
                x_in.at[1, part, row, band], x_in.at[1, part, :, band], x_in.at[1, part, others, band],
            )
            for part in parts
        ]
        for band in parts
    ]

    def x_again(band):
        for piece in pieces[2 * band:2 * band + 2]:
            wait_piece(yz_second, piece)
            unpack_banded(piece)
        for part in parts:
            start(x_third[band][part])

    def yz_again(band):
        for part in parts:
            wait(x_second[part][band])
        for piece in pieces[2 * band:2 * band + 2]:
            pack_banded(piece)
            start_piece(yz_third, piece)

    x_again(0)
    yz_again(0)
    yz_again(1)
    x_again(1)
    yz_fourth = yz_exchange(1, 1)
    x_fourth = [
        [
            x_copies(
                1, 1, part, band, lambda peer: x_res.at[1, part, peer, band],
                out.at[0, band, :, share(row, part)], out.at[0, band, :, half_blocks],
                x_res.at[1, part, others, band],
            )
            for band in parts
        ]
        for part in parts
    ]

    def columns_again(piece):
        wait_piece(yz_third, piece)
        col_filter(1, piece)
        start_piece(yz_fourth, piece)

    def rows_again(part):
        for band in parts:
            wait(x_third[band][part])
        row_filter(1, part, x_fourth[part])

    for step in SECOND_ORDER:
        (columns_again if step[0] == "c" else rows_again)(int(step[1]))
    for exchange in (yz_first, yz_second, yz_third):
        wait_sent(exchange.values())
    wait_sent(sum(x_first + x_second + x_third, []))
    for piece in pieces:
        wait_piece(yz_fourth, piece)
        unpack_natural(piece)
    for exchange in sum(x_fourth, []):
        wait(exchange)
    wait_sent(yz_fourth.values())
    wait_sent(sum(x_fourth, []))


def finish_kernel(result, out, sems):
    pieces = [
        pltpu.make_async_copy(result.at[foot, band], out.at[foot, band], sems.at[foot, band])
        for foot in range(2)
        for band in range(PARTS)
    ]
    for piece in pieces:
        piece.start()
    for piece in pieces:
        piece.wait()


def body(elevation, row_spectra, col_spectra):
    tiles = elevation.reshape(PARTS, PAIRS, 8, BLOCKS, LANES).transpose(0, 1, 3, 2, 4)
    row_lines = row_spectra.reshape(2, 2, ROWS // LANES, LANES).transpose(0, 2, 1, 3)
    col_lines = col_spectra.reshape(2, 2, SIDE * HALVES, LANES).transpose(0, 2, 1, 3)
    inputs = [
        tiles,
        row_lines.reshape(2, 2 * ROWS // LANES, LANES),
        col_lines.reshape(2, 2 * SIDE * HALVES, LANES),
    ] + [jnp.asarray(table) for table in dft_constants()]
    field = (PARTS, PAIRS, BLOCKS, 8, LANES)
    packed = (PIECES, PAIRS, PARTS, LINES, HALVES, STRIPS, LANES)
    slots = (PARTS, ROW_DEVICES, PARTS, PAIRS, SLOTS, 8, LANES)
    hbm = pl.BlockSpec(memory_space=pltpu.HBM)
    vmem = pl.BlockSpec(memory_space=pltpu.VMEM)
    result = pl.pallas_call(
        kernel,
        out_shape=pltpu.VMEM((2,) + field, jnp.float32),
        in_specs=[hbm] * len(inputs),
        out_specs=vmem,
        scratch_shapes=[pltpu.VMEM(member.shape, member.dtype) for member in inputs] + [
            pltpu.VMEM((2, 2, SIDE, SIDE), jnp.float32),
            pltpu.VMEM((2, LANES, ROWS), jnp.bfloat16),
            pltpu.VMEM((2, LANES, ROWS), jnp.bfloat16),
            pltpu.VMEM((2,) + packed, jnp.float32),
            pltpu.VMEM((2,) + packed, jnp.float32),
            pltpu.VMEM((2,) + packed, jnp.float32),
            pltpu.VMEM((2,) + packed, jnp.float32),
            pltpu.VMEM(field, jnp.float32),
            pltpu.VMEM((2,) + slots, jnp.float32),
            pltpu.VMEM((2,) + slots, jnp.float32),
            pltpu.VMEM(field, jnp.float32),
            pltpu.VMEM((2 * ROWS, SLOTS * LANES), jnp.bfloat16),
            pltpu.VMEM((2 * ROWS, SLOTS * LANES), jnp.bfloat16),
            pltpu.SemaphoreType.DMA((2, 2, PIECES)),
            pltpu.SemaphoreType.DMA((2, 2, PIECES)),
            pltpu.SemaphoreType.DMA((2, 2, PARTS, PARTS)),
            pltpu.SemaphoreType.DMA((2, 2, PARTS, PARTS)),
            pltpu.SemaphoreType.DMA((len(inputs),)),
        ],
        compiler_params=pltpu.CompilerParams(
            collective_id=0, has_side_effects=True, vmem_limit_bytes=52 * 2**20
        ),
    )(*inputs)
    result = pl.pallas_call(
        finish_kernel,
        out_shape=jax.ShapeDtypeStruct((2,) + field, jnp.float32),
        in_specs=[vmem],
        out_specs=pl.BlockSpec(memory_space=pltpu.HBM),
        scratch_shapes=[pltpu.SemaphoreType.DMA((2, PARTS))],
        compiler_params=pltpu.CompilerParams(vmem_limit_bytes=2**20),
    )(result)
    result = result.reshape(2, TILES, BLOCKS, 8, LANES)
    return result.transpose(0, 1, 3, 2, 4).reshape((2,) + elevation.shape)


def solution(mesh):
    in_specs = (P("row", "col"), P(), P())
    out_specs = P(None, "row", "col")
    return jax.shard_map(body, mesh=mesh, in_specs=in_specs, out_specs=out_specs, check_vma=False)
```

```python
import ml_dtypes
import jax
import jax.numpy as jnp
import numpy as np
from jax import lax
from jax.experimental import pallas as pl
from jax.experimental.pallas import tpu as pltpu
from jax.sharding import PartitionSpec as P

MESH = pl.DeviceIdType.MESH
SIDE = 256
LANES = 128
ROW_DEVICES = 8
COL_DEVICES = 16
ROWS = 1024
LOCAL_COLS = 4096
BLOCKS = LOCAL_COLS // LANES
TILES = ROWS // ROW_DEVICES // 8
PARTS = 2
PIECES = 4
SLOTS = BLOCKS // ROW_DEVICES // PARTS
BAND = 8 // PARTS
LINES = 8 // PIECES
HALVES = SIDE // LANES
STRIPS = LOCAL_COLS // SIDE
PAIRS = TILES // PARTS
X_CUTS = 1
GROUPS = [[(0,), (1,), (2,), (3,)]] * 3 + [[(0, 1), (2,), (3,)]]
FIRST_ORDER = ["c0", "r0", "c1", "c2", "r1", "c3"]
SECOND_ORDER = ["c0", "c1", "r0", "c2", "r1", "c3"]
YZ_STEPS = [
    (1, 1), (3, 3), (2, 2), (1, 3), (3, 1), (2, 1), (1, 2), (2, 3),
    (3, 2), (2, 0), (0, 2), (1, 0), (0, 1), (3, 0), (0, 3),
]
X_STEPS = [(1, 0), (3, 0), (1, 1), (3, 1), (2, 0), (2, 1), (0, 1)]


def split_constant(values):
    high = values.astype(ml_dtypes.bfloat16)
    low = (values - high.astype(np.float64)).astype(ml_dtypes.bfloat16)
    return [high, low]


def dft_constants():
    index = np.arange(SIDE)
    angles = 2.0 * np.pi / SIDE * (np.outer(index, index) % SIDE)
    cos, sin = np.cos(angles), np.sin(angles)
    forward = np.block([[cos, sin], [-sin, cos]])
    inverse = np.block([[cos, -sin], [sin, cos]])
    matrices = np.stack(split_constant(forward) + split_constant(inverse))
    turn = 2.0 * np.pi / (SIDE * SIDE) * np.outer(index, index)
    turns = np.stack([np.cos(turn), np.sin(turn)]).astype(np.float32)
    low = np.arange(8)
    lane = np.arange(LANES)
    first = 2.0 * np.pi / ROWS * (
        low[None, :, None] * (LANES * low[:, None, None] + lane[None, None, :]) % ROWS
    )
    first = np.stack([np.cos(first), np.sin(first)]).astype(np.float32)
    second = 2.0 * np.pi / LANES * (np.outer(lane, lane) % LANES)
    second = (np.stack([np.cos(second), np.sin(second)]) / ROWS).astype(np.float32)
    return matrices, turns, first, second


def split(values):
    high = values.astype(jnp.bfloat16)
    low = (values - high.astype(jnp.float32)).astype(jnp.bfloat16)
    return high, low


def dot(left, right):
    return jnp.dot(left, right, preferred_element_type=jnp.float32)


def dot_precise(left, right):
    return jnp.dot(
        left, right, preferred_element_type=jnp.float32, precision=lax.Precision.HIGHEST
    )


def dot_split(left, right):
    return dot(left[0], right[0]) + (dot(left[1], right[0]) + dot(left[0], right[1]))


def interleave(first, second):
    merged = []
    count = max(len(first), len(second))
    for i in range(count):
        for member in (first, second):
            merged += member[len(member) * i // count:len(member) * (i + 1) // count]
    return merged


def kernel(
    elev_hbm, row_hbm, col_hbm, matrices_hbm, turns_hbm, first_hbm, second_hbm,
    out,
    elev, row_spec, col_spec, matrices, turns, first, second, gains, circ_hi, circ_lo,
    yz_pack, yz_in, yz_res, yz_back, col_mid, x_in, x_res, row_mid, x_hi, x_lo,
    yz_send, yz_recv, x_send, x_recv, load_sem,
):
    row, col = lax.axis_index("row"), lax.axis_index("col")
    yz_peers = [
        lax.rem(col // 4 + step[0], 4) * 4 + lax.rem(col % 4 + step[1], 4) for step in YZ_STEPS
    ]
    x_peers = [
        lax.rem(row // 2 + step[0], 4) * 2 + lax.rem(row % 2 + step[1], 2) for step in X_STEPS
    ]

    barrier = pltpu.get_barrier_semaphore()
    for peer in x_peers:
        pl.semaphore_signal(barrier, inc=1, device_id=(peer, col), device_id_type=MESH)
    for peer in yz_peers:
        pl.semaphore_signal(barrier, inc=1, device_id=(row, peer), device_id_type=MESH)

    loads = [
        pltpu.make_async_copy(source, target, load_sem.at[i])
        for i, (source, target) in enumerate([
            (elev_hbm, elev), (row_hbm, row_spec), (first_hbm, first), (second_hbm, second),
            (col_hbm, col_spec), (matrices_hbm, matrices), (turns_hbm, turns),
        ])
    ]
    for load in loads:
        load.start()

    def yz_copies(half, stage, group, source, target):
        sent, received = yz_send.at[half, stage, group[0]], yz_recv.at[half, stage, group[0]]
        count = len(group)
        pieces = pl.ds(group[0], count)

        def piece_of(field, peer):
            return field.at[half, pieces, peer // PARTS, peer % PARTS]

        copies = [
            pltpu.make_async_remote_copy(
                src_ref=piece_of(source, peer), dst_ref=piece_of(target, col), send_sem=sent,
                recv_sem=received, device_id=(row, peer), device_id_type=MESH,
            )
            for peer in yz_peers
        ]
        arrived = target.at[half, pieces]
        shares = source.at[half, pieces].reshape(count * COL_DEVICES, LINES * HALVES, STRIPS, LANES)
        leaving = shares.at[pl.ds(0, count * (COL_DEVICES - 1))]
        return (
            copies, pltpu.make_async_copy(piece_of(source, col), piece_of(target, col), received),
            pltpu.make_async_copy(arrived, arrived, received), pltpu.make_async_copy(leaving, leaving, sent),
        )

    def x_copies(half, stage, part, band, source, target, arrived, leaving):
        sent, received = x_send.at[half, stage, part, band], x_recv.at[half, stage, part, band]
        cuts = [pl.ds(cut * PAIRS // X_CUTS, PAIRS // X_CUTS) for cut in range(X_CUTS)]
        copies = [
            pltpu.make_async_remote_copy(
                src_ref=source(peer).at[cut], dst_ref=target.at[cut], send_sem=sent, recv_sem=received,
                device_id=(peer, col), device_id_type=MESH,
            )
            for peer in x_peers
            for cut in cuts
        ]
        return (
            copies, pltpu.make_async_copy(source(row), target, received),
            pltpu.make_async_copy(arrived, arrived, received), pltpu.make_async_copy(leaving, leaving, sent),
        )

    def start(exchange):
        for copy in exchange[0] + [exchange[1]]:
            copy.start()

    def wait(exchange):
        exchange[2].wait()

    def wait_sent(exchanges):
        for exchange in exchanges:
            exchange[3].wait()

    def natural(piece):
        for line in range(LINES):
            for side in range(HALVES):
                yield line, side, pl.ds(8 * side + LINES * piece + line, SIDE, stride=8 * HALVES)

    def banded(piece):
        begin = LINES * piece % BAND
        for turn in range(PARTS):
            for line in range(LINES):
                for side in range(HALVES):
                    where = pl.ds(8 * side + BAND * turn + begin + line, SIDE // PARTS, stride=8 * HALVES)
                    yield turn, line, side, where

    def pack_natural(piece):
        rows = elev.reshape(SIDE * 8 * HALVES, LANES)
        for line, side, where in natural(piece):
            yz_pack[0, piece, :, :, line, side] = rows[where, :].reshape(PAIRS, PARTS, STRIPS, LANES)

    def pack_banded(piece):
        rows = row_mid.at[LINES * piece // BAND].reshape(PAIRS * BLOCKS * 8, LANES)
        for turn, line, side, where in banded(piece):
            yz_pack[1, piece, :, turn, line, side] = rows[where, :].reshape(PAIRS, STRIPS, LANES)

    def unpack_banded(piece):
        rows = col_mid.at[LINES * piece // BAND].reshape(PAIRS * BLOCKS * 8, LANES)
        for turn, line, side, where in banded(piece):
            rows[where, :] = yz_back[0, piece, :, turn, line, side].reshape(SIDE // PARTS, LANES)

    def unpack_natural(piece):
        rows = out.at[1].reshape(SIDE * 8 * HALVES, LANES)
        for line, side, where in natural(piece):
            rows[where, :] = yz_back[1, piece, :, :, line, side].reshape(SIDE, LANES)

    def build_circulant(foot):
        real = row_spec[foot, pl.ds(0, 8, stride=2), :]
        imag = row_spec[foot, pl.ds(1, 8, stride=2), :]
        turned_real = jnp.zeros((8, LANES), jnp.float32)
        turned_imag = jnp.zeros((8, LANES), jnp.float32)
        for i in range(8):
            cos, sin = first[0, i], first[1, i]
            turned_real += real[i:i + 1] * cos + imag[i:i + 1] * sin
            turned_imag += imag[i:i + 1] * cos - real[i:i + 1] * sin
        grid = dot_precise(turned_real, second[0]) + dot_precise(turned_imag, second[1])
        index = lax.broadcasted_iota(jnp.int32, (LANES, ROWS), 1)
        group = lax.broadcasted_iota(jnp.int32, (LANES, ROWS), 0)
        spread = dot_precise(grid, jnp.where(index // 8 == group, 1.0, 0.0))
        keep = index[:8] % 8 == group[:8]
        profile = jnp.sum(jnp.where(keep, spread, 0.0), axis=0, keepdims=True)
        rolled = pltpu.roll(jnp.broadcast_to(profile, (LANES, ROWS)), 0, 1, stride=1, stride_axis=0)
        banded_row = lax.broadcasted_iota(jnp.int32, (LANES, LANES), 0)
        natural_row = lax.broadcasted_iota(jnp.int32, (LANES, LANES), 1)
        source = banded_row % 64 // BAND * 8 + banded_row // 64 * BAND + banded_row % BAND
        for target, values in zip((circ_hi, circ_lo), split(rolled)):
            if foot == 1:
                order = jnp.where(source == natural_row, 1.0, 0.0).astype(jnp.bfloat16)
                target[foot] = dot(order, values).astype(jnp.bfloat16)
            else:
                source_column = natural_row % 64 // BAND * 8 + natural_row // 64 * BAND + natural_row % BAND
                order = jnp.where(source_column == banded_row, 1.0, 0.0).astype(jnp.bfloat16)
                for block in range(ROW_DEVICES):
                    lanes = slice(block * LANES, (block + 1) * LANES)
                    target[foot, :, lanes] = dot(values[:, lanes], order).astype(jnp.bfloat16)

    def build_gains(foot):
        for member in range(2):
            for side in range(HALVES):
                values = col_spec[foot, pl.ds(2 * side + member, SIDE, stride=4), :]
                gains[foot, member, side * LANES:(side + 1) * LANES, :] = values.T * (1.0 / (SIDE * SIDE))

    def row_filter(half, part, exchanges):
        foot = 1 - half
        for slot in range(SLOTS):
            lanes = slice(slot * LANES, (slot + 1) * LANES)
            high, low = split(x_in[half, part, :, :, :, slot].reshape(ROWS, LANES))
            for base in (0, ROWS):
                x_hi[base:base + ROWS, lanes] = high
                x_lo[base:base + ROWS, lanes] = low
        for i, owner in enumerate(x_peers + [row]):
            rows = pl.ds(pl.multiple_of(owner * LANES, LANES), ROWS)
            result = dot_split((circ_hi[foot], circ_lo[foot]), (x_hi[rows, :], x_lo[rows, :]))
            for slot in range(SLOTS):
                x_res[half, part, owner, :, :, slot] = result[:, slot * LANES:(slot + 1) * LANES].reshape(
                    PARTS, PAIRS, 8, LANES
                )
            copies = exchanges[0][0][i * X_CUTS:(i + 1) * X_CUTS]
            for copy in copies if i < len(x_peers) else [exchanges[0][1]]:
                copy.start()
        for exchange in exchanges[1:]:
            start(exchange)

    def col_filter(half, piece):
        foot = half
        forward = (matrices[0], matrices[1])
        inverse = (matrices[2], matrices[3])
        cos, sin = turns[0], turns[1]
        gain_real, gain_imag = gains[foot, 0], gains[foot, 1]

        def load_line(line):
            return jnp.concatenate(
                [yz_in[half, piece, :, :, line, side].reshape(SIDE, LANES) for side in range(HALVES)], 1
            )

        def store_line(line, values):
            for side in range(HALVES):
                yz_res[half, piece, :, :, line, side] = values[:, side * LANES:(side + 1) * LANES].reshape(
                    PAIRS, PARTS, STRIPS, LANES
                )

        for line in range(0, LINES, 2):
            field = jnp.concatenate([load_line(line), load_line(line + 1)], 0)
            result = dot_split(forward, split(field))
            real, imag = result[:SIDE], result[SIDE:]
            field = jnp.concatenate([real * cos + imag * sin, imag * cos - real * sin], 1)
            result = dot_split(split(field), inverse)
            real, imag = result[:, :SIDE], result[:, SIDE:]
            field = jnp.concatenate(
                [real * gain_real - imag * gain_imag, real * gain_imag + imag * gain_real], 1
            )
            result = dot_split(split(field), forward)
            real, imag = result[:, :SIDE], result[:, SIDE:]
            field = jnp.concatenate([real * cos - imag * sin, imag * cos + real * sin], 0)
            result = dot_split(inverse, split(field))
            store_line(line, result[:SIDE])
            store_line(line + 1, result[SIDE:])

    def share(owner, part):
        return pl.ds(SLOTS * (PARTS * owner + part), SLOTS)

    def yz_exchange(half, stage):
        source, target = ((yz_pack, yz_in), (yz_res, yz_back))[stage]
        return {group: yz_copies(half, stage, group, source, target) for group in GROUPS[2 * half + stage]}

    def wait_piece(exchange, piece):
        for group in exchange:
            if group[0] == piece:
                wait(exchange[group])

    def start_piece(exchange, piece):
        for group in exchange:
            if group[-1] == piece:
                start(exchange[group])

    parts = range(PARTS)
    pieces = range(PIECES)
    others = pl.ds(0, ROW_DEVICES - 1)
    half_blocks = pl.ds(0, BLOCKS // PARTS)

    yz_first = yz_exchange(0, 0)
    x_first = [
        [
            x_copies(
                0, 0, part, band, lambda peer: elev.at[band, :, share(peer, part)],
                x_in.at[0, part, row, band], x_in.at[0, part, :, band], x_in.at[0, part, others, band],
            )
            for band in parts
        ]
        for part in parts
    ]
    loads[0].wait()
    for piece in pieces[:2]:
        pack_natural(piece)
    pl.semaphore_wait(barrier, len(YZ_STEPS) + len(X_STEPS))
    for part in parts:
        members = [yz_first[group] for group in yz_first if group[0] // 2 == part]
        for copy in interleave(
            sum((member[0] for member in members), []), x_first[part][0][0] + x_first[part][1][0]
        ):
            copy.start()
        for exchange in members + x_first[part]:
            exchange[1].start()
        if part == 0:
            for piece in pieces[2:]:
                pack_natural(piece)
    for load in loads[1:]:
        load.wait()
    for foot in range(2):
        build_circulant(foot)
        build_gains(foot)
    yz_second = yz_exchange(0, 1)
    x_second = [
        [
            x_copies(
                0, 1, part, band, lambda peer: x_res.at[0, part, peer, band],
                row_mid.at[band, :, share(row, part)], row_mid.at[band, :, half_blocks],
                x_res.at[0, part, others, band],
            )
            for band in parts
        ]
        for part in parts
    ]

    def rows_once(part):
        for band in parts:
            wait(x_first[part][band])
        row_filter(0, part, x_second[part])

    def columns_once(piece):
        wait_piece(yz_first, piece)
        col_filter(0, piece)
        start_piece(yz_second, piece)

    for step in FIRST_ORDER:
        (columns_once if step[0] == "c" else rows_once)(int(step[1]))

    yz_third = yz_exchange(1, 0)
    x_third = [
        [
            x_copies(
                1, 0, part, band, lambda peer: col_mid.at[band, :, share(peer, part)],
                x_in.at[1, part, row, band], x_in.at[1, part, :, band], x_in.at[1, part, others, band],
            )
            for part in parts
        ]
        for band in parts
    ]

    def x_again(band):
        for piece in pieces[2 * band:2 * band + 2]:
            wait_piece(yz_second, piece)
            unpack_banded(piece)
        for part in parts:
            start(x_third[band][part])

    def yz_again(band):
        for part in parts:
            wait(x_second[part][band])
        for piece in pieces[2 * band:2 * band + 2]:
            pack_banded(piece)
            start_piece(yz_third, piece)

    x_again(0)
    yz_again(0)
    yz_again(1)
    x_again(1)
    yz_fourth = yz_exchange(1, 1)
    x_fourth = [
        [
            x_copies(
                1, 1, part, band, lambda peer: x_res.at[1, part, peer, band],
                out.at[0, band, :, share(row, part)], out.at[0, band, :, half_blocks],
                x_res.at[1, part, others, band],
            )
            for band in parts
        ]
        for part in parts
    ]

    def columns_again(piece):
        wait_piece(yz_third, piece)
        col_filter(1, piece)
        start_piece(yz_fourth, piece)

    def rows_again(part):
        for band in parts:
            wait(x_third[band][part])
        row_filter(1, part, x_fourth[part])

    for step in SECOND_ORDER:
        (columns_again if step[0] == "c" else rows_again)(int(step[1]))
    for exchange in (yz_first, yz_second, yz_third):
        wait_sent(exchange.values())
    wait_sent(sum(x_first + x_second + x_third, []))
    for piece in pieces:
        wait_piece(yz_fourth, piece)
        unpack_natural(piece)
    for exchange in sum(x_fourth, []):
        wait(exchange)
    wait_sent(yz_fourth.values())
    wait_sent(sum(x_fourth, []))


def finish_kernel(result, out, sems):
    pieces = [
        pltpu.make_async_copy(result.at[foot], out.at[foot], sems.at[foot])
        for foot in range(2)
    ]
    for piece in pieces:
        piece.start()
    for piece in pieces:
        piece.wait()


def body(elevation, row_spectra, col_spectra):
    tiles = elevation.reshape(PARTS, PAIRS, 8, BLOCKS, LANES).transpose(0, 1, 3, 2, 4)
    row_lines = row_spectra.reshape(2, 2, ROWS // LANES, LANES).transpose(0, 2, 1, 3)
    col_lines = col_spectra.reshape(2, 2, SIDE * HALVES, LANES).transpose(0, 2, 1, 3)
    inputs = [
        tiles,
        row_lines.reshape(2, 2 * ROWS // LANES, LANES),
        col_lines.reshape(2, 2 * SIDE * HALVES, LANES),
    ] + [jnp.asarray(table) for table in dft_constants()]
    field = (PARTS, PAIRS, BLOCKS, 8, LANES)
    packed = (PIECES, PAIRS, PARTS, LINES, HALVES, STRIPS, LANES)
    slots = (PARTS, ROW_DEVICES, PARTS, PAIRS, SLOTS, 8, LANES)
    hbm = pl.BlockSpec(memory_space=pltpu.HBM)
    vmem = pl.BlockSpec(memory_space=pltpu.VMEM)
    result = pl.pallas_call(
        kernel,
        out_shape=pltpu.VMEM((2,) + field, jnp.float32),
        in_specs=[hbm] * len(inputs),
        out_specs=vmem,
        scratch_shapes=[pltpu.VMEM(member.shape, member.dtype) for member in inputs] + [
            pltpu.VMEM((2, 2, SIDE, SIDE), jnp.float32),
            pltpu.VMEM((2, LANES, ROWS), jnp.bfloat16),
            pltpu.VMEM((2, LANES, ROWS), jnp.bfloat16),
            pltpu.VMEM((2,) + packed, jnp.float32),
            pltpu.VMEM((2,) + packed, jnp.float32),
            pltpu.VMEM((2,) + packed, jnp.float32),
            pltpu.VMEM((2,) + packed, jnp.float32),
            pltpu.VMEM(field, jnp.float32),
            pltpu.VMEM((2,) + slots, jnp.float32),
            pltpu.VMEM((2,) + slots, jnp.float32),
            pltpu.VMEM(field, jnp.float32),
            pltpu.VMEM((2 * ROWS, SLOTS * LANES), jnp.bfloat16),
            pltpu.VMEM((2 * ROWS, SLOTS * LANES), jnp.bfloat16),
            pltpu.SemaphoreType.DMA((2, 2, PIECES)),
            pltpu.SemaphoreType.DMA((2, 2, PIECES)),
            pltpu.SemaphoreType.DMA((2, 2, PARTS, PARTS)),
            pltpu.SemaphoreType.DMA((2, 2, PARTS, PARTS)),
            pltpu.SemaphoreType.DMA((len(inputs),)),
        ],
        compiler_params=pltpu.CompilerParams(
            collective_id=0, has_side_effects=True, vmem_limit_bytes=52 * 2**20
        ),
    )(*inputs)
    result = pl.pallas_call(
        finish_kernel,
        out_shape=jax.ShapeDtypeStruct((2,) + field, jnp.float32),
        in_specs=[vmem],
        out_specs=pl.BlockSpec(memory_space=pltpu.HBM),
        scratch_shapes=[pltpu.SemaphoreType.DMA((2,))],
        compiler_params=pltpu.CompilerParams(vmem_limit_bytes=2**20),
    )(result)
    result = result.reshape(2, TILES, BLOCKS, 8, LANES)
    return result.transpose(0, 1, 3, 2, 4).reshape((2,) + elevation.shape)


def solution(mesh):
    in_specs = (P("row", "col"), P(), P())
    out_specs = P(None, "row", "col")
    return jax.shard_map(body, mesh=mesh, in_specs=in_specs, out_specs=out_specs, check_vma=False)
```
